128 devices in a mesh: ens: 8 (over y_lo, z), grid: 16 (over y_hi, x, core).
Axes of the slice: x: 4, y: 4 (y_hi: 2, y_lo: 2; y = y_hi * 2 + y_lo), z: 4, core: 2. Of those that a mesh axis runs over, the one named last changes fastest.
Arguments:
- latent: bfloat16 [8, 98304, 1024], P('ens', 'grid'), may hold values from -60 to 60
- proj_weight: bfloat16 [1024, 100], replicated, may hold values from -0.1875 to 0.1875
- truth: float32 [100, 98304], P(None, 'grid'), may hold values from -8 to 8
- area_weight: float32 [98304], P('grid'), may hold values from 0.5 to 6
- var_weight: float32 [100], replicated, may hold values from 0.2 to 2
Outputs:
- loss: float32 [], replicated
- latent_grad: bfloat16 [8, 98304, 1024], P('ens', 'grid')
- weight_grad: float32 [1024, 100], P('grid')
The draws below stay inside these ranges and needn't reach their ends.
All inputs are finite; a program needn't handle non-finite values.
Results may differ from the reference program's by a relative error of at most 0.0087.
The reference program's roundings to bfloat16 on the way (of `preds` and `grads`) count: a program that leaves them out, or rounds other values in their place, can miss the bound.
Values may be sent and summed in bfloat16 or wider, within the bound.
A program may use at most 128 MiB of HBM per device.

```python
import math
import jax
import jax.numpy as jnp
from jax import lax

LAT = 1024
VARS = 100
P_DEV = 6144
POINTS = 98304
MEMBERS = 8


def draw_latent(key, part):
    key = jax.random.fold_in(key, 11)
    first, second = jax.random.split(key, 2)
    shape = (MEMBERS, POINTS, LAT)
    base = jax.random.normal(first, shape, jnp.float32)
    member = (1.0 + 2.0 * jnp.arange(MEMBERS, dtype=jnp.float32) / (MEMBERS - 1))[:, None, None]
    blocks = POINTS // P_DEV
    pairing = jax.random.permutation(second, blocks)
    point_block = jnp.arange(POINTS) // P_DEV
    feature_block = jnp.arange(LAT) // (LAT // blocks)
    spike = jnp.where(pairing[point_block][:, None] == feature_block[None, :], 3.0, 1.0)
    value = jnp.clip(base * member * spike[None], -60.0, 60.0)
    return value.astype(jnp.bfloat16)


def draw_area_weight(key, part):
    key = jax.random.fold_in(key, 23)
    place = jnp.arange(POINTS, dtype=jnp.float32) / POINTS
    rough = jnp.exp(jax.random.uniform(key, (POINTS,), jnp.float32, 0.0, 1.0986))
    return (0.5 + 1.5 * place) * rough


def block_levels(stream_key, extent, shards, low, largest):
    gain, own = 1.0, jax.random.fold_in(stream_key, 6)
    for axis_at, shards_of in shards:
        heights = jnp.exp(jax.random.uniform(jax.random.fold_in(own, axis_at), (shards_of,), jnp.float32, low / len(shards), largest / len(shards)))
        gain = gain * jnp.repeat(heights, extent[axis_at] // shards_of).reshape([-1 if axis == axis_at else 1 for axis in range(len(extent))])
    return gain


def normal_values(key, dims, scale, reach, shards=(), kind=jnp.bfloat16):
    entries = jax.random.normal(key, dims, jnp.float32) * scale
    if len(shards) > 0:
        entries = block_levels(key, dims, shards, -0.22, 0.18) * entries
    return jnp.clip(entries, min=-reach, max=reach).astype(kind)


def setup_inputs(seed: int = 0) -> dict:
    key_list = jax.random.split(jax.random.key(seed), 6)
    return {
        "latent": draw_latent(jax.random.fold_in(key_list[5], 71), 0),
        "proj_weight": normal_values(key_list[1], (LAT, VARS), LAT ** -0.5, 0.1875),
        "truth": normal_values(key_list[2], (VARS, POINTS), 1.5, 8.0, ((1, 16),), jnp.float32),
        "area_weight": draw_area_weight(jax.random.fold_in(key_list[5], 71), 0),
        "var_weight": jnp.clip(jnp.exp(jax.random.uniform(key_list[4], (VARS,), jnp.float32, math.log(0.2), math.log(2.0))), 0.2, 2.0),
    }


delta = 0.05

def soft_abs(x):
    return jnp.sqrt(x * x + delta * delta) - delta

def soft_sign(x):
    return x / jnp.sqrt(x * x + delta * delta)

def reference(latent, proj_weight, truth, area_weight, var_weight):
    weight_wide = proj_weight.astype(jnp.float32)

    def project(hrows):
        return jnp.dot(hrows.astype(jnp.float32), weight_wide, preferred_element_type=jnp.float32).T.astype(jnp.bfloat16)
    preds = lax.map(project, latent).astype(jnp.float32)
    count = MEMBERS
    scale = var_weight[:, None] * area_weight[None, :]
    skill = jnp.zeros_like(truth)
    spread = jnp.zeros_like(truth)
    pulls = jnp.zeros_like(preds)
    for other in range(count):
        skill = skill + soft_abs(preds[other] - truth)
        diff = preds - preds[other][None]
        spread = spread + lax.optimization_barrier(jnp.sum(soft_abs(diff), axis=0))
        pulls = pulls + soft_sign(diff)
    crps = skill / count - spread / (2.0 * count * (count - 1))
    total = jnp.sum(scale * crps)
    loss = total / (POINTS * VARS)
    grads = (scale[None] * (soft_sign(preds - truth[None]) / count - pulls / (count * (count - 1)))).astype(jnp.bfloat16)

    def back(pair):
        hrows, grad_m = pair
        grad_wide = grad_m.astype(jnp.float32)
        lgrad = lax.dot_general(grad_wide, weight_wide, (((0,), (1,)), ((), ())), preferred_element_type=jnp.float32)
        wterm = lax.dot_general(hrows.astype(jnp.float32), grad_wide, (((0,), (1,)), ((), ())), preferred_element_type=jnp.float32)
        return (lgrad.astype(jnp.bfloat16), wterm)
    latent_grad, wterms = lax.map(back, (latent, grads))
    weight_grad = lax.optimization_barrier(jnp.sum(wterms, axis=0)) / jnp.sqrt(jnp.float32(POINTS * MEMBERS))
    return (loss, latent_grad, weight_grad)
```

```python
import functools
import math

import jax
import jax.numpy as jnp
from jax import lax
from jax.experimental import pallas as pl
from jax.experimental.pallas import tpu as pltpu
from jax.sharding import PartitionSpec as P

DELTA = 0.05
CHUNKS = 3
LANES = 128
ROWS = 16
MESH = pl.DeviceIdType.MESH


def score_block(members, target, scale):
    count = len(members)
    square = DELTA * DELTA
    pulls = [None] * count
    spread = None
    for a in range(count):
        for b in range(a + 1, count):
            diff = members[a] - members[b]
            inner = diff * diff + square
            inverse = lax.rsqrt(inner)
            sign = diff * inverse
            root = inner * inverse
            spread = root if spread is None else spread + root
            pulls[a] = sign if pulls[a] is None else pulls[a] + sign
            pulls[b] = -sign if pulls[b] is None else pulls[b] - sign
    skill = None
    grads = []
    for a in range(count):
        diff = members[a] - target
        inner = diff * diff + square
        inverse = lax.rsqrt(inner)
        root = inner * inverse
        skill = root if skill is None else skill + root
        sign = diff * inverse
        grads.append(scale * (sign * (1.0 / count) - pulls[a] * (1.0 / (count * (count - 1)))))
    crps = skill * (1.0 / count) - spread * (1.0 / (count * (count - 1))) - 0.5 * DELTA
    return scale * crps, grads


def kernel(
    sizes,
    latent_hbm,
    weight_ref,
    truth_hbm,
    area_ref,
    var_ref,
    out_ref,
    wgrad_ref,
    loss_ref,
    latent,
    weight,
    truth,
    var,
    psend,
    precv,
    gsend,
    grecv,
    wsum,
    asend,
    arecv,
    brecv,
    load_sem,
    truth_sem,
    psend_sem,
    precv_sem,
    gsend_sem,
    grecv_sem,
    asend_sem,
    arecv_sem,
    bsend_sem,
    brecv_sem,
):
    count, shards, points, lat, nvar = sizes
    padded = weight.shape[0]
    chunk = points // CHUNKS
    width = chunk // count
    half = count // 2
    me = lax.axis_index("ens")
    mine = lax.axis_index("grid")
    my_y, my_z = me // half, me % half

    def sent_to(slot):
        return ((my_y + slot // half) % 2) * half + (my_z + slot % half) % half

    def came_from(slot):
        return ((my_y + slot // half) % 2) * half + (my_z + half - slot % half) % half

    def load(c):
        rows = pl.ds(c * chunk, chunk)
        return pltpu.make_async_copy(latent_hbm.at[0, rows], latent.at[rows], load_sem.at[c])

    def load_truth(c):
        first = pl.multiple_of(c * chunk + me * width, LANES)
        return pltpu.make_async_copy(truth_hbm.at[:, pl.ds(first, width)], truth.at[c], truth_sem.at[c])

    for c in range(CHUNKS):
        load(c).start()
    for c in range(CHUNKS):
        load_truth(c).start()

    barrier = pltpu.get_barrier_semaphore()
    for slot in range(1, count):
        pl.semaphore_signal(barrier, inc=1, device_id={"ens": sent_to(slot)}, device_id_type=MESH)
    for step in range(1, shards):
        pl.semaphore_signal(barrier, inc=1, device_id={"grid": (mine + step) % shards}, device_id_type=MESH)

    whole = nvar // ROWS * ROWS
    weight[pl.ds(0, whole), :] = weight_ref[pl.ds(0, whole), :]
    weight[pl.ds(whole, padded - whole), :] = jnp.concatenate(
        [
            weight_ref[pl.ds(whole, nvar - whole), :].astype(jnp.float32),
            jnp.zeros((padded - nvar, lat), jnp.float32),
        ],
        axis=0,
    ).astype(jnp.bfloat16)
    row = jnp.concatenate([var_ref[...], jnp.zeros((1, LANES - nvar), jnp.float32)], axis=1)
    var[...] = jnp.broadcast_to(row, (LANES, LANES)).T
    wsum[...] = jnp.zeros_like(wsum)

    pl.semaphore_wait(barrier, count - 1 + shards - 1)

    def send_preds(c, slot):
        return pltpu.make_async_remote_copy(
            src_ref=psend.at[c, slot],
            dst_ref=precv.at[c, slot],
            send_sem=psend_sem.at[c, slot],
            recv_sem=precv_sem.at[c, slot],
            device_id={"ens": sent_to(slot)},
            device_id_type=MESH,
        )

    def send_grads(c, slot):
        lanes = pl.ds(pl.multiple_of(me * width, LANES), width)
        return pltpu.make_async_remote_copy(
            src_ref=gsend.at[c, slot],
            dst_ref=grecv.at[c, :, lanes],
            send_sem=gsend_sem.at[c, slot],
            recv_sem=grecv_sem.at[c, slot],
            device_id={"ens": came_from(slot)},
            device_id_type=MESH,
        )

    def project(c, slot):
        first = pl.multiple_of(c * chunk + sent_to(slot) * width, LANES)
        return lax.dot_general(
            weight[...],
            latent[pl.ds(first, width), :],
            (((1,), (1,)), ((), ())),
            preferred_element_type=jnp.float32,
        ).astype(jnp.bfloat16)

    for c in range(CHUNKS):
        load(c).wait()

        def forward(step, carry, c=c):
            slot = count - 1 - step
            psend[c, slot] = project(c, slot)
            send_preds(c, slot).start()
            return carry

        lax.fori_loop(0, count - 1, forward, 0)
        precv[c, 0] = project(c, 0)

    total = jnp.zeros((8, LANES), jnp.float32)
    blocks = width // LANES
    for c in range(CHUNKS):
        load_truth(c).wait()
        for slot in range(1, count):
            send_preds(c, slot).wait_recv()
        first = (c * chunk + me * width) // LANES

        def put(slot, rows, lane, value, c=c):
            if slot == 0:
                lanes = pl.ds(pl.multiple_of(me * width + lane, LANES), LANES)
                grecv[c, rows, lanes] = value
            else:
                gsend[c, slot, rows, pl.ds(lane, LANES)] = value

        def whole_rows(step, acc, c=c, first=first):
            block = step % blocks
            lane = pl.multiple_of(block * LANES, LANES)
            start = pl.multiple_of(step // blocks * ROWS, ROWS)
            rows = pl.ds(start, ROWS)
            members = [precv[c, s, rows, pl.ds(lane, LANES)].astype(jnp.float32) for s in range(count)]
            target = truth[c, rows, pl.ds(lane, LANES)]
            scale = var[rows, :] * area_ref[pl.ds(first + block, 1), :]
            terms, grads = score_block(members, target, scale)
            for s in range(count):
                put(s, rows, lane, grads[s].astype(jnp.bfloat16))
            return acc + terms[:8] + terms[8:]

        total = lax.fori_loop(0, whole // ROWS * blocks, whole_rows, total)

        def last_rows(block, acc, c=c, first=first):
            lane = pl.multiple_of(block * LANES, LANES)
            rows = pl.ds(whole, ROWS)
            members = [precv[c, s, rows, pl.ds(lane, LANES)].astype(jnp.float32)[:8] for s in range(count)]
            target = jnp.concatenate(
                [truth[c, pl.ds(whole, nvar - whole), pl.ds(lane, LANES)], jnp.zeros((8 - nvar + whole, LANES), jnp.float32)],
                axis=0,
            )
            scale = var[pl.ds(whole, 8), :] * area_ref[pl.ds(first + block, 1), :]
            terms, grads = score_block(members, target, scale)
            rest = jnp.zeros((ROWS - 8, LANES), jnp.float32)
            for s in range(count):
                put(s, rows, lane, jnp.concatenate([grads[s], rest], axis=0).astype(jnp.bfloat16))
            return acc + terms

        total = lax.fori_loop(0, blocks, last_rows, total)
        for slot in range(count - 1, 0, -1):
            send_grads(c, slot).start()
    partial = jnp.sum(total)

    cut = 256
    for c in range(CHUNKS):
        for slot in range(1, count):
            send_grads(c, slot).wait_recv()

        def weight_part(step, carry, c=c):
            lanes = pl.ds(pl.multiple_of(step * cut, cut), cut)
            wsum[pl.ds(0, padded), lanes] += jnp.dot(
                grecv[c], latent[pl.ds(c * chunk, chunk), lanes], preferred_element_type=jnp.float32
            )
            return carry

        lax.fori_loop(0, lat // cut, weight_part, 0)
        if c == CHUNKS - 1:
            wsum[pl.ds(padded, LANES - padded), :] = jnp.broadcast_to(partial, (LANES - padded, lat))
            share = lat // shards
            for block in range(lat // LANES):
                turned = wsum[:, pl.ds(block * LANES, LANES)].T
                for part in range(LANES // share):
                    asend[block * (LANES // share) + part] = turned[part * share : (part + 1) * share]
            arecv[mine] = asend[mine]
            for step in range(1, shards):
                send_share(asend, arecv, asend_sem, arecv_sem, mine, shards, step).start()

        def latent_part(step, carry, c=c):
            lanes = pl.ds(pl.multiple_of(step * cut, cut), cut)
            rows = pl.ds(pl.multiple_of(c * chunk + step * cut, cut), cut)
            out_ref[0, rows, :] = lax.dot_general(
                grecv[c, :, lanes], weight[...], (((0,), (0,)), ((), ())), preferred_element_type=jnp.float32
            ).astype(jnp.bfloat16)
            return carry

        lax.fori_loop(0, chunk // cut, latent_part, 0)

    for step in range(1, shards):
        send_share(asend, arecv, asend_sem, arecv_sem, mine, shards, step).wait_recv()
    summed = arecv[0]
    for k in range(1, shards):
        summed = summed + arecv[k]
    brecv[me] = summed
    for slot in range(1, count):
        send_sum(brecv, bsend_sem, brecv_sem, me, sent_to, slot).start()
    for slot in range(1, count):
        send_sum(brecv, bsend_sem, brecv_sem, me, sent_to, slot).wait_recv()
    final = brecv[0]
    for k in range(1, count):
        final = final + brecv[k]
    wgrad_ref[...] = final[:, :nvar] * (1.0 / math.sqrt(points * shards * count))
    loss_ref[...] = final[0:1, LANES - 1 : LANES] * (1.0 / (points * shards * nvar))

    for c in range(CHUNKS):
        for slot in range(1, count):
            send_preds(c, slot).wait_send()
            send_grads(c, slot).wait_send()
    for step in range(1, shards):
        send_share(asend, arecv, asend_sem, arecv_sem, mine, shards, step).wait_send()
    for slot in range(1, count):
        send_sum(brecv, bsend_sem, brecv_sem, me, sent_to, slot).wait_send()


def send_share(asend, arecv, send_sem, recv_sem, mine, shards, step):
    to = (mine + step) % shards
    return pltpu.make_async_remote_copy(
        src_ref=asend.at[to],
        dst_ref=arecv.at[mine],
        send_sem=send_sem.at[step],
        recv_sem=recv_sem.at[step],
        device_id={"grid": to},
        device_id_type=MESH,
    )


def send_sum(brecv, send_sem, recv_sem, me, sent_to, slot):
    return pltpu.make_async_remote_copy(
        src_ref=brecv.at[me],
        dst_ref=brecv.at[me],
        send_sem=send_sem.at[slot],
        recv_sem=recv_sem.at[slot],
        device_id={"ens": sent_to(slot)},
        device_id_type=MESH,
    )


def per_device(latent, proj_weight, truth, area_weight, var_weight):
    count, shards = lax.axis_size("ens"), lax.axis_size("grid")
    _, points, lat = latent.shape
    nvar = truth.shape[0]
    padded = -(-nvar // ROWS) * ROWS
    width = points // CHUNKS // count
    share = lat // shards
    sizes = (count, shards, points, lat, nvar)
    hbm = pl.BlockSpec(memory_space=pl.ANY)
    vmem = pl.BlockSpec(memory_space=pltpu.VMEM)
    dma = pltpu.SemaphoreType.DMA
    latent_grad, weight_grad, loss = pl.pallas_call(
        functools.partial(kernel, sizes),
        out_shape=(
            jax.ShapeDtypeStruct((1, points, lat), jnp.bfloat16),
            jax.ShapeDtypeStruct((share, nvar), jnp.float32),
            jax.ShapeDtypeStruct((1, 1), jnp.float32),
        ),
        in_specs=[hbm, vmem, hbm, vmem, vmem],
        out_specs=(vmem, vmem, vmem),
        scratch_shapes=[
            pltpu.VMEM((points, lat), jnp.bfloat16),
            pltpu.VMEM((padded, lat), jnp.bfloat16),
            pltpu.VMEM((CHUNKS, nvar, width), jnp.float32),
            pltpu.VMEM((LANES, LANES), jnp.float32),
            pltpu.VMEM((CHUNKS, count, padded, width), jnp.bfloat16),
            pltpu.VMEM((CHUNKS, count, padded, width), jnp.bfloat16),
            pltpu.VMEM((CHUNKS, count, padded, width), jnp.bfloat16),
            pltpu.VMEM((CHUNKS, padded, points // CHUNKS), jnp.bfloat16),
            pltpu.VMEM((LANES, lat), jnp.float32),
            pltpu.VMEM((shards, share, LANES), jnp.float32),
            pltpu.VMEM((shards, share, LANES), jnp.float32),
            pltpu.VMEM((count, share, LANES), jnp.float32),
            dma((CHUNKS,)),
            dma((CHUNKS,)),
            dma((CHUNKS, count)),
            dma((CHUNKS, count)),
            dma((CHUNKS, count)),
            dma((CHUNKS, count)),
            dma((shards,)),
            dma((shards,)),
            dma((count,)),
            dma((count,)),
        ],
        compiler_params=pltpu.CompilerParams(
            collective_id=0, has_side_effects=True, vmem_limit_bytes=48 * 2**20
        ),
        name="crps_step",
    )(
        latent,
        proj_weight.T,
        truth,
        area_weight.reshape(points // LANES, LANES),
        var_weight.reshape(1, nvar),
    )
    return (loss[0, 0], latent_grad, weight_grad)


def solution(mesh):
    placed = (P("ens", "grid", None), P(), P(None, "grid"), P("grid"), P())
    return jax.shard_map(
        per_device,
        mesh=mesh,
        in_specs=placed,
        out_specs=(P(), P("ens", "grid", None), P("grid", None)),
        check_vma=False,
    )
```

```python
import functools
import math

import jax
import jax.numpy as jnp
from jax import lax
from jax.experimental import pallas as pl
from jax.experimental.pallas import tpu as pltpu
from jax.sharding import PartitionSpec as P

DELTA = 0.05
CHUNKS = 3
LANES = 128
ROWS = 16
MESH = pl.DeviceIdType.MESH


def score_block(members, target, scale):
    count = len(members)
    square = DELTA * DELTA
    pulls = [None] * count
    spread = None
    for a in range(count):
        for b in range(a + 1, count):
            diff = members[a] - members[b]
            inner = diff * diff + square
            inverse = lax.rsqrt(inner)
            sign = diff * inverse
            root = inner * inverse
            spread = root if spread is None else spread + root
            pulls[a] = sign if pulls[a] is None else pulls[a] + sign
            pulls[b] = -sign if pulls[b] is None else pulls[b] - sign
    skill = None
    grads = []
    for a in range(count):
        diff = members[a] - target
        inner = diff * diff + square
        inverse = lax.rsqrt(inner)
        root = inner * inverse
        skill = root if skill is None else skill + root
        sign = diff * inverse
        grads.append(scale * (sign * (1.0 / count) - pulls[a] * (1.0 / (count * (count - 1)))))
    crps = skill * (1.0 / count) - spread * (1.0 / (count * (count - 1))) - 0.5 * DELTA
    return scale * crps, grads


def kernel(
    sizes,
    latent_hbm,
    weight_hbm,
    truth_hbm,
    area_hbm,
    var_hbm,
    out_ref,
    wgrad_ref,
    loss_ref,
    latent,
    weight_in,
    weight,
    truth,
    area,
    var_in,
    var,
    psend,
    precv,
    gsend,
    grecv,
    grads,
    wsum,
    asend,
    arecv,
    bsend,
    brecv,
    crecv,
    load_sem,
    truth_sem,
    small_sem,
    psend_sem,
    precv_sem,
    gsend_sem,
    grecv_sem,
    asend_sem,
    arecv_sem,
    bsend_sem,
    brecv_sem,
    csend_sem,
    crecv_sem,
):
    count, shards, points, lat, nvar = sizes
    padded = weight.shape[0]
    chunk = points // CHUNKS
    width = chunk // count
    blocks = width // LANES
    half = count // 2
    whole = nvar // ROWS * ROWS
    left = nvar - whole
    tail = blocks * whole
    me = lax.axis_index("ens")
    mine = lax.axis_index("grid")
    my_y, my_z = me // half, me % half
    core, spot = mine % 2, mine // 2
    spots = shards // 2
    place = my_y * spots + spot
    places = 2 * spots

    def sent_to(slot):
        return ((my_y + slot // half) % 2) * half + (my_z + slot % half) % half

    def came_from(slot):
        return ((my_y + slot // half) % 2) * half + (my_z + half - slot % half) % half

    def device_at(there):
        return {"ens": there // spots * half + my_z, "grid": there % spots * 2 + core}

    def load(c):
        rows = pl.ds(c * chunk, chunk)
        return pltpu.make_async_copy(latent_hbm.at[0, rows], latent.at[rows], load_sem.at[c])

    def load_truth(c):
        first = pl.multiple_of(c * chunk + me * width, LANES)
        return pltpu.make_async_copy(truth_hbm.at[:, pl.ds(first, width)], truth.at[c], truth_sem.at[c])

    small = [
        pltpu.make_async_copy(weight_hbm, weight_in, small_sem.at[0]),
        pltpu.make_async_copy(var_hbm, var_in, small_sem.at[1]),
        pltpu.make_async_copy(area_hbm, area, small_sem.at[2]),
    ]
    for copy in small:
        copy.start()
    for c in range(CHUNKS):
        load(c).start()
    for c in range(CHUNKS):
        load_truth(c).start()

    sibling = mine + 1 - 2 * core
    barrier = pltpu.get_barrier_semaphore()
    for slot in range(1, count):
        pl.semaphore_signal(barrier, inc=1, device_id={"ens": sent_to(slot)}, device_id_type=MESH)
    for step in range(1, places):
        pl.semaphore_signal(barrier, inc=1, device_id=device_at((place + step) % places), device_id_type=MESH)
    pl.semaphore_signal(barrier, inc=1, device_id={"grid": sibling}, device_id_type=MESH)

    for copy in small:
        copy.wait()
    weight[pl.ds(0, whole), :] = weight_in[pl.ds(0, whole), :]
    weight[pl.ds(whole, padded - whole), :] = jnp.concatenate(
        [
            weight_in[pl.ds(whole, left), :].astype(jnp.float32),
            jnp.zeros((padded - nvar, lat), jnp.float32),
        ],
        axis=0,
    ).astype(jnp.bfloat16)
    row = jnp.concatenate([var_in[...], jnp.zeros((1, LANES - nvar), jnp.float32)], axis=1)
    var[...] = jnp.broadcast_to(row, (LANES, LANES)).T

    def send_preds(c, slot):
        return pltpu.make_async_remote_copy(
            src_ref=psend.at[c, slot],
            dst_ref=precv.at[c, slot],
            send_sem=psend_sem.at[c, slot],
            recv_sem=precv_sem.at[c, slot],
            device_id={"ens": sent_to(slot)},
            device_id_type=MESH,
        )

    def send_grads(c, slot):
        return pltpu.make_async_remote_copy(
            src_ref=gsend.at[c, slot],
            dst_ref=grecv.at[c, slot],
            send_sem=gsend_sem.at[c, slot],
            recv_sem=grecv_sem.at[c, slot],
            device_id={"ens": came_from(slot)},
            device_id_type=MESH,
        )

    def send_core(step):
        some = pl.ds(step * 2, 2)
        return pltpu.make_async_remote_copy(
            src_ref=asend.at[1 - core, some],
            dst_ref=arecv.at[some],
            send_sem=asend_sem.at[step],
            recv_sem=arecv_sem.at[step],
            device_id={"grid": sibling},
            device_id_type=MESH,
        )

    def send_share(step):
        there = (place + step) % places
        rows = pl.ds(pl.multiple_of(there // spots * brecv.shape[1], 8), brecv.shape[1])
        return pltpu.make_async_remote_copy(
            src_ref=bsend.at[there % spots, rows],
            dst_ref=brecv.at[place],
            send_sem=bsend_sem.at[step],
            recv_sem=brecv_sem.at[step],
            device_id=device_at(there),
            device_id_type=MESH,
        )

    def send_sum(slot):
        return pltpu.make_async_remote_copy(
            src_ref=crecv.at[me],
            dst_ref=crecv.at[me],
            send_sem=csend_sem.at[slot],
            recv_sem=crecv_sem.at[slot],
            device_id={"ens": sent_to(slot)},
            device_id_type=MESH,
        )

    def project(target, c, slot):
        first = pl.multiple_of(c * chunk + sent_to(slot) * width, LANES)
        preds = lax.dot_general(
            weight[...],
            latent[pl.ds(first, width), :],
            (((1,), (1,)), ((), ())),
            preferred_element_type=jnp.float32,
        )
        for b in range(blocks):
            target[c, slot, pl.ds(b * whole, whole), :] = preds[:whole, b * LANES : (b + 1) * LANES].astype(jnp.bfloat16)
        rest = [preds[whole:nvar, b * LANES : (b + 1) * LANES] for b in range(blocks)]
        rest.append(jnp.zeros((ROWS - blocks * left, LANES), jnp.float32))
        target[c, slot, pl.ds(tail, ROWS), :] = jnp.concatenate(rest, axis=0).astype(jnp.bfloat16)

    for c in range(CHUNKS):
        load(c).wait()

        def forward(step, carry, c=c):
            slot = count - 1 - step
            project(psend, c, slot)
            if c == 0:

                @pl.when(step == 0)
                def _():
                    pl.semaphore_wait(barrier, count - 1 + places - 1 + 1)

            send_preds(c, slot).start()
            return carry

        lax.fori_loop(0, count - 1, forward, 0)
        project(precv, c, 0)

    total = jnp.zeros((8, LANES), jnp.float32)
    for c in range(CHUNKS):
        load_truth(c).wait()
        for slot in range(1, count):
            send_preds(c, slot).wait_recv()
        first = (c * chunk + me * width) // LANES

        def put(rows, values, c=c):
            grecv[c, 0, rows, :] = values[0].astype(jnp.bfloat16)
            for s in range(1, count):
                gsend[c, s, rows, :] = values[s].astype(jnp.bfloat16)

        def whole_rows(step, acc, c=c, first=first, put=put):
            block = step % blocks
            lanes = pl.ds(pl.multiple_of(block * LANES, LANES), LANES)
            start = pl.multiple_of(step // blocks * ROWS, ROWS)
            rows = pl.ds(pl.multiple_of(block * whole + start, ROWS), ROWS)
            members = [precv[c, s, rows, :].astype(jnp.float32) for s in range(count)]
            target = truth[c, pl.ds(start, ROWS), lanes]
            scale = var[pl.ds(start, ROWS), :] * area[pl.ds(first + block, 1), :]
            terms, pulled = score_block(members, target, scale)
            put(rows, pulled)
            return acc + terms[:8] + terms[8:]

        total = lax.fori_loop(0, whole // ROWS * blocks, whole_rows, total)

        rows = pl.ds(tail, ROWS)
        members = [precv[c, s, rows, :].astype(jnp.float32)[:8] for s in range(count)]
        spare = [jnp.zeros((8 - blocks * left, LANES), jnp.float32)] if blocks * left < 8 else []
        target = jnp.concatenate(
            [truth[c, pl.ds(whole, left), pl.ds(b * LANES, LANES)] for b in range(blocks)] + spare, axis=0
        )
        scale = jnp.concatenate(
            [var[pl.ds(whole, left), :] * area[pl.ds(first + b, 1), :] for b in range(blocks)] + spare, axis=0
        )
        terms, pulled = score_block(members, target, scale)
        rest = jnp.zeros((ROWS - 8, LANES), jnp.float32)
        put(rows, [jnp.concatenate([value, rest], axis=0) for value in pulled])
        total = total + terms
        for slot in range(count - 1, 0, -1):
            send_grads(c, slot).start()
    partial = jnp.sum(total)

    cut = 256

    def weight_part(step, c):
        lanes = pl.ds(pl.multiple_of(step * cut, cut), cut)
        part = jnp.dot(grads[...], latent[pl.ds(c * chunk, chunk), lanes], preferred_element_type=jnp.float32)
        if c == 0:
            wsum[pl.ds(0, padded), lanes] = part
        else:
            wsum[pl.ds(0, padded), lanes] += part

    def latent_part(step, c):
        lanes = pl.ds(pl.multiple_of(step * cut, cut), cut)
        rows = pl.ds(pl.multiple_of(c * chunk + step * cut, cut), cut)
        out_ref[0, rows, :] = lax.dot_general(
            grads[:, lanes], weight[...], (((0,), (0,)), ((), ())), preferred_element_type=jnp.float32
        ).astype(jnp.bfloat16)

    def loop(start, stop, body):
        def step_of(step, carry):
            body(step)
            return carry

        lax.fori_loop(start, stop, step_of, 0)

    for c in range(CHUNKS):
        for slot in range(1, count):
            send_grads(c, slot).wait_recv()

        def unpack(slot, c=c):
            at = sent_to(slot) * width
            last = grecv[c, slot, pl.ds(tail, ROWS), :].astype(jnp.float32)
            for b in range(blocks):
                lanes = pl.ds(pl.multiple_of(at + b * LANES, LANES), LANES)
                grads[pl.ds(0, whole), lanes] = grecv[c, slot, pl.ds(b * whole, whole), :]
                grads[pl.ds(whole, ROWS), lanes] = jnp.concatenate(
                    [last[b * left : (b + 1) * left], jnp.zeros((ROWS - left, LANES), jnp.float32)], axis=0
                ).astype(jnp.bfloat16)

        loop(0, count, unpack)
        if c < CHUNKS - 1:
            loop(0, lat // cut, lambda step, c=c: weight_part(step, c))
            loop(0, chunk // cut, lambda step, c=c: latent_part(step, c))

    c = CHUNKS - 1
    wsum[pl.ds(padded, LANES - padded), :] = jnp.broadcast_to(partial, (LANES - padded, lat))

    def weight_sent(step):
        weight_part(step, c)
        for b in range(cut // LANES):
            lanes = pl.ds(pl.multiple_of(step * cut + b * LANES, LANES), LANES)
            turned = wsum[:, lanes].T
            asend[0, step * 2 + b] = turned[: LANES // 2]
            asend[1, step * 2 + b] = turned[LANES // 2 :]
        send_core(step).start()

    loop(0, lat // cut, weight_sent)
    early = 2
    loop(0, early, lambda step: latent_part(step, c))
    for step in range(lat // cut):
        send_core(step).wait_recv()
    bsend[...] = asend[core] + arecv[...]
    for step in range(1, places):
        send_share(step).start()
    brecv[place] = bsend[spot, pl.ds(pl.multiple_of(my_y * brecv.shape[1], 8), brecv.shape[1]), :]
    loop(early, chunk // cut, lambda step: latent_part(step, c))
    for step in range(1, places):
        send_share(step).wait_recv()
    summed = brecv[0]
    for k in range(1, places):
        summed = summed + brecv[k]
    crecv[me] = summed
    for slot in range(1, count):
        send_sum(slot).start()
    for slot in range(1, count):
        send_sum(slot).wait_recv()
    for y in range(2):
        final = crecv[y * half]
        for k in range(1, half):
            final = final + crecv[y * half + k]
        rows = pl.ds(y * brecv.shape[1], brecv.shape[1])
        wgrad_ref[rows, :] = final[:, :nvar] * (1.0 / math.sqrt(points * shards * count))
        if y == 0:
            loss_ref[...] = final[0:1, LANES - 1 : LANES] * (1.0 / (points * shards * nvar))

    for c in range(CHUNKS):
        for slot in range(1, count):
            send_preds(c, slot).wait_send()
            send_grads(c, slot).wait_send()
    for step in range(lat // cut):
        send_core(step).wait_send()
    for step in range(1, places):
        send_share(step).wait_send()
    for slot in range(1, count):
        send_sum(slot).wait_send()


def copy_out(latent_grad, wgrad, loss, latent_out, wgrad_out, loss_out, sem):
    copy = pltpu.make_async_copy(latent_grad, latent_out, sem)
    copy.start()
    wgrad_out[...] = wgrad[...]
    loss_out[...] = loss[...]
    copy.wait()


def per_device(latent, proj_weight, truth, area_weight, var_weight):
    count, shards = lax.axis_size("ens"), lax.axis_size("grid")
    _, points, lat = latent.shape
    nvar = truth.shape[0]
    padded = -(-nvar // ROWS) * ROWS
    width = points // CHUNKS // count
    packed = width // LANES * (nvar // ROWS * ROWS) + ROWS
    share = lat // shards
    sizes = (count, shards, points, lat, nvar)
    hbm = pl.BlockSpec(memory_space=pltpu.HBM)
    vmem = pl.BlockSpec(memory_space=pltpu.VMEM)
    dma = pltpu.SemaphoreType.DMA
    out_shape = (
        jax.ShapeDtypeStruct((1, points, lat), jnp.bfloat16),
        jax.ShapeDtypeStruct((share, nvar), jnp.float32),
        jax.ShapeDtypeStruct((1, 1), jnp.float32),
    )
    results = pl.pallas_call(
        functools.partial(kernel, sizes),
        out_shape=(pltpu.VMEM((1, points, lat), jnp.bfloat16), *out_shape[1:]),
        in_specs=[hbm] * 5,
        out_specs=(vmem, vmem, vmem),
        scratch_shapes=[
            pltpu.VMEM((points, lat), jnp.bfloat16),
            pltpu.VMEM((nvar, lat), jnp.bfloat16),
            pltpu.VMEM((padded, lat), jnp.bfloat16),
            pltpu.VMEM((CHUNKS, nvar, width), jnp.float32),
            pltpu.VMEM((points // LANES, LANES), jnp.float32),
            pltpu.VMEM((1, nvar), jnp.float32),
            pltpu.VMEM((LANES, LANES), jnp.float32),
            pltpu.VMEM((CHUNKS, count, packed, LANES), jnp.bfloat16),
            pltpu.VMEM((CHUNKS, count, packed, LANES), jnp.bfloat16),
            pltpu.VMEM((CHUNKS, count, packed, LANES), jnp.bfloat16),
            pltpu.VMEM((CHUNKS, count, packed, LANES), jnp.bfloat16),
            pltpu.VMEM((padded, points // CHUNKS), jnp.bfloat16),
            pltpu.VMEM((LANES, lat), jnp.float32),
            pltpu.VMEM((2, shards // 2, share, LANES), jnp.float32),
            pltpu.VMEM((shards // 2, share, LANES), jnp.float32),
            pltpu.VMEM((shards // 2, share, LANES), jnp.float32),
            pltpu.VMEM((shards, share // 2, LANES), jnp.float32),
            pltpu.VMEM((count, share // 2, LANES), jnp.float32),
            dma((CHUNKS,)),
            dma((CHUNKS,)),
            dma((3,)),
            dma((CHUNKS, count)),
            dma((CHUNKS, count)),
            dma((CHUNKS, count)),
            dma((CHUNKS, count)),
            dma((lat // 256,)),
            dma((lat // 256,)),
            dma((shards,)),
            dma((shards,)),
            dma((count,)),
            dma((count,)),
        ],
        compiler_params=pltpu.CompilerParams(
            collective_id=0, has_side_effects=True, vmem_limit_bytes=36 * 2**20
        ),
        name="crps_step",
    )(
        *(
            pltpu.with_memory_space_constraint(x, pltpu.HBM)
            for x in (
                latent,
                proj_weight.T,
                truth,
                area_weight.reshape(points // LANES, LANES),
                var_weight.reshape(1, nvar),
            )
        )
    )
    latent_grad, weight_grad, loss = pl.pallas_call(
        copy_out,
        out_shape=out_shape,
        in_specs=[vmem, vmem, vmem],
        out_specs=(hbm, vmem, vmem),
        scratch_shapes=[dma],
        compiler_params=pltpu.CompilerParams(vmem_limit_bytes=2**20),
        name="copy_out",
    )(pltpu.with_memory_space_constraint(results[0], pltpu.VMEM), *results[1:])
    return (loss[0, 0], latent_grad, weight_grad)


def solution(mesh):
    placed = (P("ens", "grid", None), P(), P(None, "grid"), P("grid"), P())
    return jax.shard_map(
        per_device,
        mesh=mesh,
        in_specs=placed,
        out_specs=(P(), P("ens", "grid", None), P("grid", None)),
        check_vma=False,
    )
```

```python
import functools
import math

import jax
import jax.numpy as jnp
from jax import lax
from jax.experimental import pallas as pl
from jax.experimental.pallas import tpu as pltpu
from jax.sharding import PartitionSpec as P

DELTA = 0.05
CHUNKS = 3
LANES = 128
ROWS = 16
MESH = pl.DeviceIdType.MESH


def score_block(members, target, scale):
    count = len(members)
    square = DELTA * DELTA
    pulls = [None] * count
    spread = None
    for a in range(count):
        for b in range(a + 1, count):
            diff = members[a] - members[b]
            inner = diff * diff + square
            inverse = lax.rsqrt(inner)
            sign = diff * inverse
            root = inner * inverse
            spread = root if spread is None else spread + root
            pulls[a] = sign if pulls[a] is None else pulls[a] + sign
            pulls[b] = -sign if pulls[b] is None else pulls[b] - sign
    skill = None
    grads = []
    for a in range(count):
        diff = members[a] - target
        inner = diff * diff + square
        inverse = lax.rsqrt(inner)
        root = inner * inverse
        skill = root if skill is None else skill + root
        sign = diff * inverse
        grads.append(scale * (sign * (1.0 / count) - pulls[a] * (1.0 / (count * (count - 1)))))
    crps = skill * (1.0 / count) - spread * (1.0 / (count * (count - 1))) - 0.5 * DELTA
    return scale * crps, grads


def kernel(
    sizes,
    latent_hbm,
    weight_hbm,
    truth_hbm,
    area_hbm,
    var_hbm,
    out_ref,
    summed_ref,
    latent,
    weight_in,
    weight,
    truth,
    area,
    var_in,
    var,
    psend,
    precv,
    gsend,
    grecv,
    grads,
    wsum,
    asend,
    arecv,
    bsend,
    brecv,
    crecv,
    load_sem,
    first_sem,
    truth_sem,
    small_sem,
    psend_sem,
    precv_sem,
    gsend_sem,
    grecv_sem,
    asend_sem,
    arecv_sem,
    bsend_sem,
    brecv_sem,
    csend_sem,
    crecv_sem,
):
    count, shards, points, lat, nvar = sizes
    padded = weight.shape[0]
    chunk = points // CHUNKS
    width = chunk // count
    blocks = width // LANES
    half = count // 2
    whole = nvar // ROWS * ROWS
    left = nvar - whole
    tail = blocks * whole
    me = lax.axis_index("ens")
    mine = lax.axis_index("grid")
    my_y, my_z = lax.div(me, half), lax.rem(me, half)
    core, spot = lax.rem(mine, 2), lax.div(mine, 2)
    spots = shards // 2
    place = my_y * spots + spot
    places = 2 * spots

    def member(slot, way):
        y, z = (slot // half, slot % half) if isinstance(slot, int) else (lax.div(slot, half), lax.rem(slot, half))
        return lax.rem(my_y + y, 2) * half + lax.rem(my_z + half + way * z, half)

    def sent_to(slot):
        return member(slot, 1)

    def came_from(slot):
        return member(slot, -1)

    def turn(step):
        if isinstance(step, int):
            return (1 - step % 2) * half + (2, 3, 1, 0)[step // 2]
        pair = lax.div(step, 2)
        return (1 - lax.rem(step, 2)) * half + 2 + pair - lax.div(pair, 2) * (2 * pair - 1)

    def device_at(there):
        y, there = there
        return {"ens": y * half + my_z, "grid": there * 2 + core}

    def partner(step):
        far = (2, 1, 3, 0)
        x = lax.rem(lax.rem(spot, 4) + far[(step - 1) // 4], 4)
        y = lax.rem(lax.div(spot, 4) * 2 + my_y + far[(step - 1) % 4], 4)
        return lax.rem(y, 2), lax.div(y, 2) * 4 + x

    def load(c):
        rows = pl.ds(c * chunk, chunk)
        return pltpu.make_async_copy(latent_hbm.at[0, rows], latent.at[rows], load_sem.at[c])

    def load_first(slot):
        rows = pl.ds(pl.multiple_of(sent_to(slot) * width, LANES), width)
        return pltpu.make_async_copy(latent_hbm.at[0, rows], latent.at[rows], first_sem.at[slot])

    def load_truth(c):
        first = pl.multiple_of(c * chunk + me * width, LANES)
        return pltpu.make_async_copy(truth_hbm.at[:, pl.ds(first, width)], truth.at[c], truth_sem.at[c])

    sibling = mine + 1 - 2 * core
    barrier = pltpu.get_barrier_semaphore()
    for slot in range(1, count):
        pl.semaphore_signal(barrier, inc=1, device_id={"ens": sent_to(slot)}, device_id_type=MESH)
    for step in range(1, places):
        pl.semaphore_signal(barrier, inc=1, device_id=device_at(partner(step)), device_id_type=MESH)
    pl.semaphore_signal(barrier, inc=1, device_id={"grid": sibling}, device_id_type=MESH)

    small = [
        pltpu.make_async_copy(weight_hbm, weight_in, small_sem.at[0]),
        pltpu.make_async_copy(var_hbm, var_in, small_sem.at[1]),
        pltpu.make_async_copy(area_hbm, area, small_sem.at[2]),
    ]
    small[0].start()
    for step in range(count):
        load_first(turn(step)).start()
    for copy in small[1:]:
        copy.start()
    small[0].wait()
    weight[pl.ds(0, whole), :] = weight_in[pl.ds(0, whole), :]
    weight[pl.ds(whole, padded - whole), :] = jnp.concatenate(
        [
            weight_in[pl.ds(whole, left), :].astype(jnp.float32),
            jnp.zeros((padded - nvar, lat), jnp.float32),
        ],
        axis=0,
    ).astype(jnp.bfloat16)

    def send_preds(c, slot):
        return pltpu.make_async_remote_copy(
            src_ref=psend.at[c, slot],
            dst_ref=precv.at[c, slot],
            send_sem=psend_sem.at[c, slot],
            recv_sem=precv_sem.at[c, slot],
            device_id={"ens": sent_to(slot)},
            device_id_type=MESH,
        )

    def send_grads(c, slot):
        return pltpu.make_async_remote_copy(
            src_ref=gsend.at[c, slot],
            dst_ref=grecv.at[c, slot],
            send_sem=gsend_sem.at[c, slot],
            recv_sem=grecv_sem.at[c, slot],
            device_id={"ens": came_from(slot)},
            device_id_type=MESH,
        )

    def send_core(step):
        some = pl.ds(step * 2, 2)
        return pltpu.make_async_remote_copy(
            src_ref=asend.at[1 - core, some],
            dst_ref=arecv.at[some],
            send_sem=asend_sem.at[step],
            recv_sem=arecv_sem.at[step],
            device_id={"grid": sibling},
            device_id_type=MESH,
        )

    def send_share(step):
        y, there = partner(step)
        rows = pl.ds(pl.multiple_of(y * brecv.shape[1], 8), brecv.shape[1])
        return pltpu.make_async_remote_copy(
            src_ref=bsend.at[there, rows],
            dst_ref=brecv.at[place],
            send_sem=bsend_sem.at[step],
            recv_sem=brecv_sem.at[step],
            device_id=device_at((y, there)),
            device_id_type=MESH,
        )

    def send_sum(slot):
        return pltpu.make_async_remote_copy(
            src_ref=crecv.at[me],
            dst_ref=crecv.at[me],
            send_sem=csend_sem.at[slot],
            recv_sem=crecv_sem.at[slot],
            device_id={"ens": sent_to(slot)},
            device_id_type=MESH,
        )

    def project(target, c, slot):
        first = pl.multiple_of(c * chunk + sent_to(slot) * width, LANES)
        preds = lax.dot_general(
            weight[...],
            latent[pl.ds(first, width), :],
            (((1,), (1,)), ((), ())),
            preferred_element_type=jnp.float32,
        )
        for b in range(blocks):
            target[c, slot, pl.ds(b * whole, whole), :] = preds[:whole, b * LANES : (b + 1) * LANES].astype(jnp.bfloat16)
        rest = [preds[whole:nvar, b * LANES : (b + 1) * LANES] for b in range(blocks)]
        rest.append(jnp.zeros((ROWS - blocks * left, LANES), jnp.float32))
        target[c, slot, pl.ds(tail, ROWS), :] = jnp.concatenate(rest, axis=0).astype(jnp.bfloat16)

    for c in range(CHUNKS):
        if c > 0:
            load(c).wait()

        def forward(step, carry, c=c):
            slot = turn(step)
            if c == 0:
                load_first(slot).wait()
            project(psend, c, slot)
            if c == 0:

                @pl.when(step == 0)
                def _():
                    pl.semaphore_wait(barrier, count - 1 + places - 1 + 1)
                    for later in range(1, CHUNKS):
                        load(later).start()
                    for later in range(CHUNKS):
                        load_truth(later).start()

            send_preds(c, slot).start()
            return carry

        lax.fori_loop(0, count - 1, forward, 0)
        if c == 0:
            load_first(0).wait()
        project(precv, c, 0)

    for copy in small[1:]:
        copy.wait()
    row = jnp.concatenate([var_in[...], jnp.zeros((1, LANES - nvar), jnp.float32)], axis=1)
    var[...] = jnp.broadcast_to(row, (LANES, LANES)).T

    total = jnp.zeros((8, LANES), jnp.float32)
    for c in range(CHUNKS):
        load_truth(c).wait()
        for slot in range(1, count):
            send_preds(c, slot).wait_recv()
        first = c * chunk // LANES + me * blocks

        def put(rows, values, c=c):
            grecv[c, 0, rows, :] = values[0].astype(jnp.bfloat16)
            for s in range(1, count):
                gsend[c, s, rows, :] = values[s].astype(jnp.bfloat16)

        def whole_rows(step, acc, c=c, first=first, put=put):
            block = lax.rem(step, blocks)
            lanes = pl.ds(pl.multiple_of(block * LANES, LANES), LANES)
            start = pl.multiple_of(lax.div(step, blocks) * ROWS, ROWS)
            rows = pl.ds(pl.multiple_of(block * whole + start, ROWS), ROWS)
            members = [precv[c, s, rows, :].astype(jnp.float32) for s in range(count)]
            target = truth[c, pl.ds(start, ROWS), lanes]
            scale = var[pl.ds(start, ROWS), :] * area[pl.ds(first + block, 1), :]
            terms, pulled = score_block(members, target, scale)
            put(rows, pulled)
            return acc + terms[:8] + terms[8:]

        total = lax.fori_loop(0, whole // ROWS * blocks, whole_rows, total)

        rows = pl.ds(tail, ROWS)
        members = [precv[c, s, rows, :].astype(jnp.float32)[:8] for s in range(count)]
        spare = [jnp.zeros((8 - blocks * left, LANES), jnp.float32)] if blocks * left < 8 else []
        target = jnp.concatenate(
            [truth[c, pl.ds(whole, left), pl.ds(b * LANES, LANES)] for b in range(blocks)] + spare, axis=0
        )
        scale = jnp.concatenate(
            [var[pl.ds(whole, left), :] * area[pl.ds(first + b, 1), :] for b in range(blocks)] + spare, axis=0
        )
        terms, pulled = score_block(members, target, scale)
        rest = jnp.zeros((ROWS - 8, LANES), jnp.float32)
        put(rows, [jnp.concatenate([value, rest], axis=0) for value in pulled])
        total = total + terms
        for step in range(count - 1):
            send_grads(c, turn(step)).start()
    partial = jnp.sum(total)

    cut = 256

    def weight_part(step, c, first=0, length=chunk):
        lanes = pl.ds(pl.multiple_of(step * cut, cut), cut)
        first = pl.multiple_of(first, LANES)
        part = jnp.dot(
            grads[:, pl.ds(first, length)],
            latent[pl.ds(pl.multiple_of(c * chunk + first, LANES), length), lanes],
            preferred_element_type=jnp.float32,
        )
        if c == 0:
            wsum[pl.ds(0, padded), lanes] = part
        else:
            wsum[pl.ds(0, padded), lanes] += part

    def latent_part(step, c):
        lanes = pl.ds(pl.multiple_of(step * cut, cut), cut)
        rows = pl.ds(pl.multiple_of(c * chunk + step * cut, cut), cut)
        out_ref[0, rows, :] = lax.dot_general(
            grads[:, lanes], weight[...], (((0,), (0,)), ((), ())), preferred_element_type=jnp.float32
        ).astype(jnp.bfloat16)

    def loop(start, stop, body):
        def step_of(step, carry):
            body(step)
            return carry

        lax.fori_loop(start, stop, step_of, 0)

    def unpack(slot, c):
        at = sent_to(slot) * width
        last = grecv[c, slot, pl.ds(tail, ROWS), :].astype(jnp.float32)
        for b in range(blocks):
            lanes = pl.ds(pl.multiple_of(at + b * LANES, LANES), LANES)
            grads[pl.ds(0, whole), lanes] = grecv[c, slot, pl.ds(b * whole, whole), :]
            grads[pl.ds(whole, ROWS), lanes] = jnp.concatenate(
                [last[b * left : (b + 1) * left], jnp.zeros((ROWS - left, LANES), jnp.float32)], axis=0
            ).astype(jnp.bfloat16)

    for c in range(CHUNKS - 1):
        for slot in range(1, count):
            send_grads(c, slot).wait_recv()
        loop(0, count, lambda slot, c=c: unpack(slot, c))
        loop(0, lat // cut, lambda step, c=c: weight_part(step, c))
        loop(0, chunk // cut, lambda step, c=c: latent_part(step, c))

    c = CHUNKS - 1
    side = half * width
    for slot in range(half, count):
        send_grads(c, slot).wait_recv()
    loop(half, count, lambda slot: unpack(slot, c))
    loop(0, lat // cut, lambda step: weight_part(step, c, (1 - my_y) * side, side))
    for slot in range(1, half):
        send_grads(c, slot).wait_recv()
    loop(0, half, lambda slot: unpack(slot, c))

    wsum[pl.ds(padded, LANES - padded), :] = jnp.broadcast_to(partial, (LANES - padded, lat))

    def weight_sent(step):
        weight_part(step, c, my_y * side, side)
        for b in range(cut // LANES):
            lanes = pl.ds(pl.multiple_of(step * cut + b * LANES, LANES), LANES)
            turned = wsum[:, lanes].T
            asend[0, step * 2 + b] = turned[: LANES // 2]
            asend[1, step * 2 + b] = turned[LANES // 2 :]
        send_core(step).start()

    loop(0, lat // cut, weight_sent)
    for step in range(lat // cut):
        send_core(step).wait_recv()
    bsend[...] = asend[core] + arecv[...]
    for step in range(1, places):
        send_share(step).start()
    brecv[place] = bsend[spot, pl.ds(pl.multiple_of(my_y * brecv.shape[1], 8), brecv.shape[1]), :]
    loop(0, chunk // cut, lambda step: latent_part(step, c))
    for c in range(CHUNKS):
        for slot in range(1, count):
            send_preds(c, slot).wait_send()
            send_grads(c, slot).wait_send()
    for step in range(lat // cut):
        send_core(step).wait_send()
    for step in range(1, places):
        send_share(step).wait_recv()
    summed = brecv[0]
    for k in range(1, places):
        summed = summed + brecv[k]
    crecv[me] = summed
    for slot in range(1, count):
        send_sum(slot).start()
    for step in range(1, places):
        send_share(step).wait_send()
    for slot in range(1, count):
        send_sum(slot).wait_recv()
    for y in range(2):
        final = crecv[y * half]
        for k in range(1, half):
            final = final + crecv[y * half + k]
        summed_ref[pl.ds(y * brecv.shape[1], brecv.shape[1]), :] = final

    for slot in range(1, count):
        send_sum(slot).wait_send()


def copy_out(sizes, latent_grad, summed, latent_out, wgrad_out, loss_out, wgrad, loss, sem):
    count, shards, points, lat, nvar = sizes
    copies = [
        pltpu.make_async_copy(latent_grad, latent_out, sem.at[0]),
        pltpu.make_async_copy(wgrad, wgrad_out, sem.at[1]),
        pltpu.make_async_copy(loss, loss_out, sem.at[2]),
    ]
    copies[0].start()
    wgrad[...] = summed[:, :nvar] * (1.0 / math.sqrt(points * shards * count))
    loss[...] = summed[0:1, LANES - 1 : LANES] * (1.0 / (points * shards * nvar))
    for copy in copies[1:]:
        copy.start()
    for copy in copies:
        copy.wait()


def per_device(latent, proj_weight, truth, area_weight, var_weight):
    count, shards = lax.axis_size("ens"), lax.axis_size("grid")
    _, points, lat = latent.shape
    nvar = truth.shape[0]
    padded = -(-nvar // ROWS) * ROWS
    width = points // CHUNKS // count
    packed = width // LANES * (nvar // ROWS * ROWS) + ROWS
    share = lat // shards
    sizes = (count, shards, points, lat, nvar)
    hbm = pl.BlockSpec(memory_space=pltpu.HBM)
    vmem = pl.BlockSpec(memory_space=pltpu.VMEM)
    dma = pltpu.SemaphoreType.DMA
    out_shape = (
        jax.ShapeDtypeStruct((1, points, lat), jnp.bfloat16),
        jax.ShapeDtypeStruct((share, nvar), jnp.float32),
        jax.ShapeDtypeStruct((1, 1), jnp.float32),
    )
    latent_grad, summed = pl.pallas_call(
        functools.partial(kernel, sizes),
        out_shape=(pltpu.VMEM((1, points, lat), jnp.bfloat16), pltpu.VMEM((share, LANES), jnp.float32)),
        in_specs=[hbm] * 5,
        out_specs=(vmem, vmem),
        scratch_shapes=[
            pltpu.VMEM((points, lat), jnp.bfloat16),
            pltpu.VMEM((nvar, lat), jnp.bfloat16),
            pltpu.VMEM((padded, lat), jnp.bfloat16),
            pltpu.VMEM((CHUNKS, nvar, width), jnp.float32),
            pltpu.VMEM((points // LANES, LANES), jnp.float32),
            pltpu.VMEM((1, nvar), jnp.float32),
            pltpu.VMEM((LANES, LANES), jnp.float32),
            pltpu.VMEM((CHUNKS, count, packed, LANES), jnp.bfloat16),
            pltpu.VMEM((CHUNKS, count, packed, LANES), jnp.bfloat16),
            pltpu.VMEM((CHUNKS, count, packed, LANES), jnp.bfloat16),
            pltpu.VMEM((CHUNKS, count, packed, LANES), jnp.bfloat16),
            pltpu.VMEM((padded, points // CHUNKS), jnp.bfloat16),
            pltpu.VMEM((LANES, lat), jnp.float32),
            pltpu.VMEM((2, shards // 2, share, LANES), jnp.float32),
            pltpu.VMEM((shards // 2, share, LANES), jnp.float32),
            pltpu.VMEM((shards // 2, share, LANES), jnp.float32),
            pltpu.VMEM((shards, share // 2, LANES), jnp.float32),
            pltpu.VMEM((count, share // 2, LANES), jnp.float32),
            dma((CHUNKS,)),
            dma((count,)),
            dma((CHUNKS,)),
            dma((3,)),
            dma((CHUNKS, count)),
            dma((CHUNKS, count)),
            dma((CHUNKS, count)),
            dma((CHUNKS, count)),
            dma((lat // 256,)),
            dma((lat // 256,)),
            dma((shards,)),
            dma((shards,)),
            dma((count,)),
            dma((count,)),
        ],
        compiler_params=pltpu.CompilerParams(
            collective_id=0, has_side_effects=True, vmem_limit_bytes=36 * 2**20
        ),
        name="crps_step",
    )(
        *(
            pltpu.with_memory_space_constraint(x, pltpu.HBM)
            for x in (
                latent,
                proj_weight.T,
                truth,
                area_weight.reshape(points // LANES, LANES),
                var_weight.reshape(1, nvar),
            )
        )
    )
    latent_grad, weight_grad, loss = pl.pallas_call(
        functools.partial(copy_out, sizes),
        out_shape=out_shape,
        in_specs=[vmem, vmem],
        out_specs=(hbm, hbm, hbm),
        scratch_shapes=[
            pltpu.VMEM((share, nvar), jnp.float32),
            pltpu.VMEM((1, 1), jnp.float32),
            dma((3,)),
        ],
        compiler_params=pltpu.CompilerParams(vmem_limit_bytes=2**20),
        name="copy_out",
    )(*(pltpu.with_memory_space_constraint(x, pltpu.VMEM) for x in (latent_grad, summed)))
    return (loss[0, 0], latent_grad, weight_grad)


def solution(mesh):
    placed = (P("ens", "grid", None), P(), P(None, "grid"), P("grid"), P())
    return jax.shard_map(
        per_device,
        mesh=mesh,
        in_specs=placed,
        out_specs=(P(), P("ens", "grid", None), P("grid", None)),
        check_vma=False,
    )
```

```python
import functools
import math

import jax
import jax.numpy as jnp
from jax import lax
from jax.experimental import pallas as pl
from jax.experimental.pallas import tpu as pltpu
from jax.sharding import PartitionSpec as P

DELTA = 0.05
CHUNKS = 3
LANES = 128
ROWS = 16
MESH = pl.DeviceIdType.MESH


def score_block(members, target, scale):
    count = len(members)
    square = DELTA * DELTA
    pulls = [None] * count
    spread = None
    for a in range(count):
        for b in range(a + 1, count):
            diff = members[a] - members[b]
            inner = diff * diff + square
            inverse = lax.rsqrt(inner)
            sign = diff * inverse
            root = inner * inverse
            spread = root if spread is None else spread + root
            pulls[a] = sign if pulls[a] is None else pulls[a] + sign
            pulls[b] = -sign if pulls[b] is None else pulls[b] - sign
    skill = None
    grads = []
    for a in range(count):
        diff = members[a] - target
        inner = diff * diff + square
        inverse = lax.rsqrt(inner)
        root = inner * inverse
        skill = root if skill is None else skill + root
        sign = diff * inverse
        grads.append(scale * (sign * (1.0 / count) - pulls[a] * (1.0 / (count * (count - 1)))))
    crps = skill * (1.0 / count) - spread * (1.0 / (count * (count - 1))) - 0.5 * DELTA
    return scale * crps, grads


def kernel(
    sizes,
    latent_hbm,
    weight_hbm,
    truth_hbm,
    area_hbm,
    var_hbm,
    out_ref,
    summed_ref,
    latent,
    weight_in,
    weight,
    truth,
    area,
    var_in,
    var,
    psend,
    precv,
    gsend,
    grecv,
    grads,
    wsum,
    asend,
    arecv,
    bsend,
    brecv,
    crecv,
    load_sem,
    first_sem,
    truth_sem,
    small_sem,
    psend_sem,
    precv_sem,
    gsend_sem,
    grecv_sem,
    asend_sem,
    arecv_sem,
    bsend_sem,
    brecv_sem,
    csend_sem,
    crecv_sem,
):
    count, shards, points, lat, nvar = sizes
    padded = weight.shape[0]
    chunk = points // CHUNKS
    width = chunk // count
    blocks = width // LANES
    half = count // 2
    whole = nvar // ROWS * ROWS
    left = nvar - whole
    tail = blocks * whole
    me = lax.axis_index("ens")
    mine = lax.axis_index("grid")
    my_y, my_z = lax.div(me, half), lax.rem(me, half)
    core, spot = lax.rem(mine, 2), lax.div(mine, 2)
    spots = shards // 2
    places = 2 * spots

    def member(slot, way):
        y, z = (slot // half, slot % half) if isinstance(slot, int) else (lax.div(slot, half), lax.rem(slot, half))
        return lax.rem(my_y + y, 2) * half + lax.rem(my_z + half + way * z, half)

    def sent_to(slot):
        return member(slot, 1)

    def came_from(slot):
        return member(slot, -1)

    def turn(step):
        if isinstance(step, int):
            return (1 - step % 2) * half + (2, 3, 1, 0)[step // 2]
        pair = lax.div(step, 2)
        return (1 - lax.rem(step, 2)) * half + 2 + pair - lax.div(pair, 2) * (2 * pair - 1)

    def device_at(there):
        y, there = there
        return {"ens": y * half + my_z, "grid": there * 2 + core}

    def partner(step):
        far = (2, 1, 3, 0)
        x = lax.rem(lax.rem(spot, 4) + far[(step - 1) // 4], 4)
        y = lax.rem(lax.div(spot, 4) * 2 + my_y + far[(step - 1) % 4], 4)
        return lax.rem(y, 2), lax.div(y, 2) * 4 + x

    def load(c):
        rows = pl.ds(c * chunk, chunk)
        return pltpu.make_async_copy(latent_hbm.at[0, rows], latent.at[rows], load_sem.at[c])

    def load_first(slot):
        rows = pl.ds(pl.multiple_of(sent_to(slot) * width, LANES), width)
        return pltpu.make_async_copy(latent_hbm.at[0, rows], latent.at[rows], first_sem.at[slot])

    def load_truth(c):
        first = pl.multiple_of(c * chunk + me * width, LANES)
        return pltpu.make_async_copy(truth_hbm.at[:, pl.ds(first, width)], truth.at[c], truth_sem.at[c])

    sibling = mine + 1 - 2 * core
    barrier = pltpu.get_barrier_semaphore()
    for slot in range(1, count):
        pl.semaphore_signal(barrier, inc=1, device_id={"ens": sent_to(slot)}, device_id_type=MESH)
    for step in range(1, places):
        pl.semaphore_signal(barrier, inc=1, device_id=device_at(partner(step)), device_id_type=MESH)
    pl.semaphore_signal(barrier, inc=1, device_id={"grid": sibling}, device_id_type=MESH)

    small = [
        pltpu.make_async_copy(weight_hbm, weight_in, small_sem.at[0]),
        pltpu.make_async_copy(var_hbm, var_in, small_sem.at[1]),
        pltpu.make_async_copy(area_hbm, area, small_sem.at[2]),
    ]
    small[0].start()
    for step in range(count):
        load_first(turn(step)).start()
    for copy in small[1:]:
        copy.start()
    small[0].wait()
    weight[pl.ds(0, whole), :] = weight_in[pl.ds(0, whole), :]
    weight[pl.ds(whole, padded - whole), :] = jnp.concatenate(
        [
            weight_in[pl.ds(whole, left), :].astype(jnp.float32),
            jnp.zeros((padded - nvar, lat), jnp.float32),
        ],
        axis=0,
    ).astype(jnp.bfloat16)

    def send_preds(c, slot):
        return pltpu.make_async_remote_copy(
            src_ref=psend.at[c, slot],
            dst_ref=precv.at[c, slot],
            send_sem=psend_sem.at[c],
            recv_sem=precv_sem.at[c],
            device_id={"ens": sent_to(slot)},
            device_id_type=MESH,
        )

    def send_grads(c, slot):
        return pltpu.make_async_remote_copy(
            src_ref=gsend.at[c, slot],
            dst_ref=grecv.at[c, slot],
            send_sem=gsend_sem.at[c],
            recv_sem=grecv_sem.at[c, lax.div(slot, half) if not isinstance(slot, int) else slot // half],
            device_id={"ens": came_from(slot)},
            device_id_type=MESH,
        )

    def send_core(step):
        some = pl.ds(step * 2, 2)
        return pltpu.make_async_remote_copy(
            src_ref=asend.at[1 - core, some],
            dst_ref=arecv.at[some],
            send_sem=asend_sem,
            recv_sem=arecv_sem,
            device_id={"grid": sibling},
            device_id_type=MESH,
        )

    def send_share(step):
        y, there = partner(step)
        rows = pl.ds(pl.multiple_of(y * brecv.shape[1], 8), brecv.shape[1])
        return pltpu.make_async_remote_copy(
            src_ref=bsend.at[there, rows],
            dst_ref=brecv.at[step - 1],
            send_sem=bsend_sem,
            recv_sem=brecv_sem,
            device_id=device_at((y, there)),
            device_id_type=MESH,
        )

    def send_sum(slot):
        return pltpu.make_async_remote_copy(
            src_ref=crecv.at[0],
            dst_ref=crecv.at[slot],
            send_sem=csend_sem,
            recv_sem=crecv_sem,
            device_id={"ens": sent_to(slot)},
            device_id_type=MESH,
        )

    def all_of(some, sem):
        return pltpu.make_async_copy(some, some, sem)

    def blocks_of(ref, c, start, stop, sem):
        return all_of(ref.at[c, pl.ds(start, stop - start)], sem)

    def project(target, c, slot):
        first = pl.multiple_of(c * chunk + sent_to(slot) * width, LANES)
        preds = lax.dot_general(
            weight[...],
            latent[pl.ds(first, width), :],
            (((1,), (1,)), ((), ())),
            preferred_element_type=jnp.float32,
        )
        for b in range(blocks):
            target[c, slot, pl.ds(b * whole, whole), :] = preds[:whole, b * LANES : (b + 1) * LANES].astype(jnp.bfloat16)
        rest = [preds[whole:nvar, b * LANES : (b + 1) * LANES] for b in range(blocks)]
        rest.append(jnp.zeros((ROWS - blocks * left, LANES), jnp.float32))
        target[c, slot, pl.ds(tail, ROWS), :] = jnp.concatenate(rest, axis=0).astype(jnp.bfloat16)

    for c in range(CHUNKS):
        if c > 0:
            load(c).wait()

        def forward(step, carry, c=c):
            slot = turn(step)
            if c == 0:
                load_first(slot).wait()
            project(psend, c, slot)
            if c == 0:

                @pl.when(step == 0)
                def _():
                    pl.semaphore_wait(barrier, count - 1 + places - 1 + 1)
                    for later in range(1, CHUNKS):
                        load(later).start()
                    for later in range(CHUNKS):
                        load_truth(later).start()

            send_preds(c, slot).start()
            return carry

        lax.fori_loop(0, count - 1, forward, 0)
        if c == 0:
            load_first(0).wait()
        project(precv, c, 0)

    for copy in small[1:]:
        copy.wait()
    row = jnp.concatenate([var_in[...], jnp.zeros((1, LANES - nvar), jnp.float32)], axis=1)
    var[...] = jnp.broadcast_to(row, (LANES, LANES)).T

    total = jnp.zeros((8, LANES), jnp.float32)
    for c in range(CHUNKS):
        load_truth(c).wait()
        blocks_of(precv, c, 1, count, precv_sem.at[c]).wait()
        first = c * chunk // LANES + me * blocks

        def put(rows, values, c=c):
            grecv[c, 0, rows, :] = values[0].astype(jnp.bfloat16)
            for s in range(1, count):
                gsend[c, s, rows, :] = values[s].astype(jnp.bfloat16)

        def whole_rows(step, acc, c=c, first=first, put=put):
            block = lax.rem(step, blocks)
            lanes = pl.ds(pl.multiple_of(block * LANES, LANES), LANES)
            start = pl.multiple_of(lax.div(step, blocks) * ROWS, ROWS)
            rows = pl.ds(pl.multiple_of(block * whole + start, ROWS), ROWS)
            members = [precv[c, s, rows, :].astype(jnp.float32) for s in range(count)]
            target = truth[c, pl.ds(start, ROWS), lanes]
            scale = var[pl.ds(start, ROWS), :] * area[pl.ds(first + block, 1), :]
            terms, pulled = score_block(members, target, scale)
            put(rows, pulled)
            return acc + terms[:8] + terms[8:]

        total = lax.fori_loop(0, whole // ROWS * blocks, whole_rows, total)

        rows = pl.ds(tail, ROWS)
        members = [precv[c, s, rows, :].astype(jnp.float32)[:8] for s in range(count)]
        spare = [jnp.zeros((8 - blocks * left, LANES), jnp.float32)] if blocks * left < 8 else []
        target = jnp.concatenate(
            [truth[c, pl.ds(whole, left), pl.ds(b * LANES, LANES)] for b in range(blocks)] + spare, axis=0
        )
        scale = jnp.concatenate(
            [var[pl.ds(whole, left), :] * area[pl.ds(first + b, 1), :] for b in range(blocks)] + spare, axis=0
        )
        terms, pulled = score_block(members, target, scale)
        rest = jnp.zeros((ROWS - 8, LANES), jnp.float32)
        put(rows, [jnp.concatenate([value, rest], axis=0) for value in pulled])
        total = total + terms
        for step in range(count - 1):
            send_grads(c, turn(step)).start()
    partial = jnp.sum(total)

    cut = 256

    def weight_part(step, c, first=0, length=chunk):
        lanes = pl.ds(pl.multiple_of(step * cut, cut), cut)
        first = pl.multiple_of(first, LANES)
        part = jnp.dot(
            grads[:, pl.ds(first, length)],
            latent[pl.ds(pl.multiple_of(c * chunk + first, LANES), length), lanes],
            preferred_element_type=jnp.float32,
        )
        if c == 0:
            wsum[pl.ds(0, padded), lanes] = part
        else:
            wsum[pl.ds(0, padded), lanes] += part

    def latent_part(step, c):
        lanes = pl.ds(pl.multiple_of(step * cut, cut), cut)
        rows = pl.ds(pl.multiple_of(c * chunk + step * cut, cut), cut)
        out_ref[0, rows, :] = lax.dot_general(
            grads[:, lanes], weight[...], (((0,), (0,)), ((), ())), preferred_element_type=jnp.float32
        ).astype(jnp.bfloat16)

    def loop(start, stop, body):
        def step_of(step, carry):
            body(step)
            return carry

        lax.fori_loop(start, stop, step_of, 0)

    def unpack(slot, c):
        at = sent_to(slot) * width
        last = grecv[c, slot, pl.ds(tail, ROWS), :].astype(jnp.float32)
        for b in range(blocks):
            lanes = pl.ds(pl.multiple_of(at + b * LANES, LANES), LANES)
            grads[pl.ds(0, whole), lanes] = grecv[c, slot, pl.ds(b * whole, whole), :]
            grads[pl.ds(whole, ROWS), lanes] = jnp.concatenate(
                [last[b * left : (b + 1) * left], jnp.zeros((ROWS - left, LANES), jnp.float32)], axis=0
            ).astype(jnp.bfloat16)

    for c in range(CHUNKS - 1):
        blocks_of(grecv, c, half, count, grecv_sem.at[c, 1]).wait()
        blocks_of(grecv, c, 1, half, grecv_sem.at[c, 0]).wait()
        loop(0, count, lambda slot, c=c: unpack(slot, c))
        loop(0, lat // cut, lambda step, c=c: weight_part(step, c))
        loop(0, chunk // cut, lambda step, c=c: latent_part(step, c))

    c = CHUNKS - 1
    side = half * width
    blocks_of(grecv, c, half, count, grecv_sem.at[c, 1]).wait()
    loop(half, count, lambda slot: unpack(slot, c))
    loop(0, lat // cut, lambda step: weight_part(step, c, (1 - my_y) * side, side))
    blocks_of(grecv, c, 1, half, grecv_sem.at[c, 0]).wait()
    loop(0, half, lambda slot: unpack(slot, c))

    wsum[pl.ds(padded, LANES - padded), :] = jnp.broadcast_to(partial, (LANES - padded, lat))

    def weight_sent(step):
        weight_part(step, c, my_y * side, side)
        for b in range(cut // LANES):
            lanes = pl.ds(pl.multiple_of(step * cut + b * LANES, LANES), LANES)
            turned = wsum[:, lanes].T
            asend[0, step * 2 + b] = turned[: LANES // 2]
            asend[1, step * 2 + b] = turned[LANES // 2 :]
        send_core(step).start()

    loop(0, lat // cut, weight_sent)
    all_of(arecv, arecv_sem).wait()
    bsend[...] = asend[core] + arecv[...]
    for step in range(1, places):
        send_share(step).start()
    brecv[places - 1] = bsend[spot, pl.ds(pl.multiple_of(my_y * brecv.shape[1], 8), brecv.shape[1]), :]
    loop(0, chunk // cut, lambda step: latent_part(step, c))
    for c in range(CHUNKS):
        blocks_of(psend, c, 1, count, psend_sem.at[c]).wait()
        blocks_of(gsend, c, 1, count, gsend_sem.at[c]).wait()
    all_of(asend.at[1 - core], asend_sem).wait()
    all_of(brecv.at[pl.ds(0, places - 1)], brecv_sem).wait()

    def share_from(x, y):
        ways = (
            lax.rem(lax.rem(spot, 4) + 4 - x, 4),
            lax.rem(lax.div(spot, 4) * 2 + my_y + 4 - y, 4),
        )
        x, y = ((1 - lax.div(d, 2)) * (3 - 2 * d) + lax.div(d, 2) * (2 * d - 4) for d in ways)
        return brecv[x * 4 + y]

    summed = share_from(0, 0)
    for k in range(1, places):
        summed = summed + share_from(k // 4, k % 4)
    crecv[0] = summed
    for slot in range(1, count):
        send_sum(slot).start()
    all_of(brecv.at[pl.ds(0, places - 1)], bsend_sem).wait()
    all_of(crecv.at[pl.ds(1, count - 1)], crecv_sem).wait()
    for y in range(2):
        side_at = lax.rem(my_y + y, 2) * half
        final = crecv[side_at + my_z]
        for k in range(1, half):
            final = final + crecv[side_at + lax.rem(my_z + half - k, half)]
        summed_ref[pl.ds(y * brecv.shape[1], brecv.shape[1]), :] = final

    all_of(crecv.at[pl.ds(1, count - 1)], csend_sem).wait()


def copy_out(sizes, latent_grad, summed, latent_out, wgrad_out, loss_out, wgrad, loss, sem):
    count, shards, points, lat, nvar = sizes
    copies = [
        pltpu.make_async_copy(latent_grad, latent_out, sem.at[0]),
        pltpu.make_async_copy(wgrad, wgrad_out, sem.at[1]),
        pltpu.make_async_copy(loss, loss_out, sem.at[2]),
    ]
    copies[0].start()
    wgrad[...] = summed[:, :nvar] * (1.0 / math.sqrt(points * shards * count))
    loss[...] = summed[0:1, LANES - 1 : LANES] * (1.0 / (points * shards * nvar))
    for copy in copies[1:]:
        copy.start()
    for copy in copies:
        copy.wait()


def per_device(latent, proj_weight, truth, area_weight, var_weight):
    count, shards = lax.axis_size("ens"), lax.axis_size("grid")
    _, points, lat = latent.shape
    nvar = truth.shape[0]
    padded = -(-nvar // ROWS) * ROWS
    width = points // CHUNKS // count
    packed = width // LANES * (nvar // ROWS * ROWS) + ROWS
    share = lat // shards
    sizes = (count, shards, points, lat, nvar)
    hbm = pl.BlockSpec(memory_space=pltpu.HBM)
    vmem = pl.BlockSpec(memory_space=pltpu.VMEM)
    dma = pltpu.SemaphoreType.DMA
    out_shape = (
        jax.ShapeDtypeStruct((1, points, lat), jnp.bfloat16),
        jax.ShapeDtypeStruct((share, nvar), jnp.float32),
        jax.ShapeDtypeStruct((1, 1), jnp.float32),
    )
    latent_grad, summed = pl.pallas_call(
        functools.partial(kernel, sizes),
        out_shape=(pltpu.VMEM((1, points, lat), jnp.bfloat16), pltpu.VMEM((share, LANES), jnp.float32)),
        in_specs=[hbm] * 5,
        out_specs=(vmem, vmem),
        scratch_shapes=[
            pltpu.VMEM((points, lat), jnp.bfloat16),
            pltpu.VMEM((nvar, lat), jnp.bfloat16),
            pltpu.VMEM((padded, lat), jnp.bfloat16),
            pltpu.VMEM((CHUNKS, nvar, width), jnp.float32),
            pltpu.VMEM((points // LANES, LANES), jnp.float32),
            pltpu.VMEM((1, nvar), jnp.float32),
            pltpu.VMEM((LANES, LANES), jnp.float32),
            pltpu.VMEM((CHUNKS, count, packed, LANES), jnp.bfloat16),
            pltpu.VMEM((CHUNKS, count, packed, LANES), jnp.bfloat16),
            pltpu.VMEM((CHUNKS, count, packed, LANES), jnp.bfloat16),
            pltpu.VMEM((CHUNKS, count, packed, LANES), jnp.bfloat16),
            pltpu.VMEM((padded, points // CHUNKS), jnp.bfloat16),
            pltpu.VMEM((LANES, lat), jnp.float32),
            pltpu.VMEM((2, shards // 2, share, LANES), jnp.float32),
            pltpu.VMEM((shards // 2, share, LANES), jnp.float32),
            pltpu.VMEM((shards // 2, share, LANES), jnp.float32),
            pltpu.VMEM((shards, share // 2, LANES), jnp.float32),
            pltpu.VMEM((count, share // 2, LANES), jnp.float32),
            dma((CHUNKS,)),
            dma((count,)),
            dma((CHUNKS,)),
            dma((3,)),
            dma((CHUNKS,)),
            dma((CHUNKS,)),
            dma((CHUNKS,)),
            dma((CHUNKS, 2)),
            dma,
            dma,
            dma,
            dma,
            dma,
            dma,
        ],
        compiler_params=pltpu.CompilerParams(
            collective_id=0, has_side_effects=True, vmem_limit_bytes=36 * 2**20
        ),
        name="crps_step",
    )(
        *(
            pltpu.with_memory_space_constraint(x, pltpu.HBM)
            for x in (
                latent,
                proj_weight.T,
                truth,
                area_weight.reshape(points // LANES, LANES),
                var_weight.reshape(1, nvar),
            )
        )
    )
    latent_grad, weight_grad, loss = pl.pallas_call(
        functools.partial(copy_out, sizes),
        out_shape=out_shape,
        in_specs=[vmem, vmem],
        out_specs=(hbm, hbm, hbm),
        scratch_shapes=[
            pltpu.VMEM((share, nvar), jnp.float32),
            pltpu.VMEM((1, 1), jnp.float32),
            dma((3,)),
        ],
        compiler_params=pltpu.CompilerParams(vmem_limit_bytes=2**20),
        name="copy_out",
    )(*(pltpu.with_memory_space_constraint(x, pltpu.VMEM) for x in (latent_grad, summed)))
    return (loss[0, 0], latent_grad, weight_grad)


def solution(mesh):
    placed = (P("ens", "grid", None), P(), P(None, "grid"), P("grid"), P())
    return jax.shard_map(
        per_device,
        mesh=mesh,
        in_specs=placed,
        out_specs=(P(), P("ens", "grid", None), P("grid", None)),
        check_vma=False,
    )
```

```python
import functools
import math

import jax
import jax.numpy as jnp
from jax import lax
from jax.experimental import pallas as pl
from jax.experimental.pallas import tpu as pltpu
from jax.sharding import PartitionSpec as P

DELTA = 0.05
CHUNKS = 3
LANES = 128
ORDER = (3, 1, 2, 7, 5, 6, 4)
ROWS = 16
MESH = pl.DeviceIdType.MESH


def score_block(members, target, scale):
    count = len(members)
    square = DELTA * DELTA
    pulls = [None] * count
    spread = None
    for a in range(count):
        for b in range(a + 1, count):
            diff = members[a] - members[b]
            inner = diff * diff + square
            inverse = lax.rsqrt(inner)
            sign = diff * inverse
            root = inner * inverse
            spread = root if spread is None else spread + root
            pulls[a] = sign if pulls[a] is None else pulls[a] + sign
            pulls[b] = -sign if pulls[b] is None else pulls[b] - sign
    skill = None
    grads = []
    for a in range(count):
        diff = members[a] - target
        inner = diff * diff + square
        inverse = lax.rsqrt(inner)
        root = inner * inverse
        skill = root if skill is None else skill + root
        sign = diff * inverse
        grads.append(scale * (sign * (1.0 / count) - pulls[a] * (1.0 / (count * (count - 1)))))
    crps = skill * (1.0 / count) - spread * (1.0 / (count * (count - 1))) - 0.5 * DELTA
    return scale * crps, grads


def kernel(
    sizes,
    latent_hbm,
    weight_hbm,
    truth_hbm,
    area_hbm,
    var_hbm,
    out_ref,
    summed_ref,
    latent,
    weight_in,
    weight,
    truth,
    area,
    var_in,
    var,
    psend,
    precv,
    gsend,
    grecv,
    grads,
    wsum,
    asend,
    arecv,
    bsend,
    brecv,
    crecv,
    load_sem,
    first_sem,
    truth_sem,
    small_sem,
    psend_sem,
    precv_sem,
    gsend_sem,
    grecv_sem,
    asend_sem,
    arecv_sem,
    bsend_sem,
    brecv_sem,
    csend_sem,
    crecv_sem,
):
    count, shards, points, lat, nvar = sizes
    padded = weight.shape[0]
    chunk = points // CHUNKS
    width = chunk // count
    blocks = width // LANES
    half = count // 2
    whole = nvar // ROWS * ROWS
    left = nvar - whole
    tail = blocks * whole
    me = lax.axis_index("ens")
    mine = lax.axis_index("grid")
    my_y, my_z = lax.div(me, half), lax.rem(me, half)
    core, spot = lax.rem(mine, 2), lax.div(mine, 2)
    spots = shards // 2
    places = 2 * spots

    def member(slot, way):
        y, z = (slot // half, slot % half) if isinstance(slot, int) else (lax.div(slot, half), lax.rem(slot, half))
        return lax.rem(my_y + y, 2) * half + lax.rem(my_z + half + way * z, half)

    def sent_to(slot):
        return member(slot, 1)

    def came_from(slot):
        return member(slot, -1)

    def device_at(there):
        y, there = there
        return {"ens": y * half + my_z, "grid": there * 2 + core}

    def partner(step):
        far = (2, 1, 3, 0)
        x = lax.rem(lax.rem(spot, 4) + far[(step - 1) // 4], 4)
        y = lax.rem(lax.div(spot, 4) * 2 + my_y + far[(step - 1) % 4], 4)
        return lax.rem(y, 2), lax.div(y, 2) * 4 + x

    def load(c):
        rows = pl.ds(c * chunk, chunk)
        return pltpu.make_async_copy(latent_hbm.at[0, rows], latent.at[rows], load_sem.at[c])

    def load_first(slot):
        rows = pl.ds(pl.multiple_of(sent_to(slot) * width, LANES), width)
        return pltpu.make_async_copy(latent_hbm.at[0, rows], latent.at[rows], first_sem.at[slot])

    def load_truth(c):
        first = pl.multiple_of(c * chunk + me * width, LANES)
        return pltpu.make_async_copy(truth_hbm.at[:, pl.ds(first, width)], truth.at[c], truth_sem.at[c])

    sibling = mine + 1 - 2 * core
    barrier = pltpu.get_barrier_semaphore()
    for slot in range(1, count):
        pl.semaphore_signal(barrier, inc=1, device_id={"ens": sent_to(slot)}, device_id_type=MESH)
    for step in range(1, places):
        pl.semaphore_signal(barrier, inc=1, device_id=device_at(partner(step)), device_id_type=MESH)
    pl.semaphore_signal(barrier, inc=1, device_id={"grid": sibling}, device_id_type=MESH)

    small = [
        pltpu.make_async_copy(weight_hbm, weight_in, small_sem.at[0]),
        pltpu.make_async_copy(var_hbm, var_in, small_sem.at[1]),
        pltpu.make_async_copy(area_hbm, area, small_sem.at[2]),
    ]
    small[0].start()
    for slot in (*ORDER, 0):
        load_first(slot).start()
    for copy in small[1:]:
        copy.start()
    small[0].wait()
    weight[pl.ds(0, whole), :] = weight_in[pl.ds(0, whole), :]
    weight[pl.ds(whole, padded - whole), :] = jnp.concatenate(
        [
            weight_in[pl.ds(whole, left), :].astype(jnp.float32),
            jnp.zeros((padded - nvar, lat), jnp.float32),
        ],
        axis=0,
    ).astype(jnp.bfloat16)

    def send_preds(c, slot):
        return pltpu.make_async_remote_copy(
            src_ref=psend.at[c, slot],
            dst_ref=precv.at[c, slot],
            send_sem=psend_sem.at[c],
            recv_sem=precv_sem.at[c],
            device_id={"ens": sent_to(slot)},
            device_id_type=MESH,
        )

    def send_grads(c, slot):
        return pltpu.make_async_remote_copy(
            src_ref=gsend.at[c, slot],
            dst_ref=grecv.at[c, slot],
            send_sem=gsend_sem.at[c],
            recv_sem=grecv_sem.at[c, lax.div(slot, half) if not isinstance(slot, int) else slot // half],
            device_id={"ens": came_from(slot)},
            device_id_type=MESH,
        )

    def send_core(step):
        some = pl.ds(step * 2, 2)
        return pltpu.make_async_remote_copy(
            src_ref=asend.at[1 - core, some],
            dst_ref=arecv.at[some],
            send_sem=asend_sem,
            recv_sem=arecv_sem,
            device_id={"grid": sibling},
            device_id_type=MESH,
        )

    def send_share(step):
        y, there = partner(step)
        rows = pl.ds(pl.multiple_of(y * brecv.shape[1], 8), brecv.shape[1])
        return pltpu.make_async_remote_copy(
            src_ref=bsend.at[there, rows],
            dst_ref=brecv.at[step - 1],
            send_sem=bsend_sem,
            recv_sem=brecv_sem,
            device_id=device_at((y, there)),
            device_id_type=MESH,
        )

    def send_sum(slot):
        return pltpu.make_async_remote_copy(
            src_ref=crecv.at[0],
            dst_ref=crecv.at[slot],
            send_sem=csend_sem,
            recv_sem=crecv_sem,
            device_id={"ens": sent_to(slot)},
            device_id_type=MESH,
        )

    def all_of(some, sem):
        return pltpu.make_async_copy(some, some, sem)

    def blocks_of(ref, c, start, stop, sem):
        return all_of(ref.at[c, pl.ds(start, stop - start)], sem)

    def project(target, c, slot):
        first = pl.multiple_of(c * chunk + sent_to(slot) * width, LANES)
        preds = lax.dot_general(
            weight[...],
            latent[pl.ds(first, width), :],
            (((1,), (1,)), ((), ())),
            preferred_element_type=jnp.float32,
        )
        for b in range(blocks):
            target[c, slot, pl.ds(b * whole, whole), :] = preds[:whole, b * LANES : (b + 1) * LANES].astype(jnp.bfloat16)
        rest = [preds[whole:nvar, b * LANES : (b + 1) * LANES] for b in range(blocks)]
        rest.append(jnp.zeros((ROWS - blocks * left, LANES), jnp.float32))
        target[c, slot, pl.ds(tail, ROWS), :] = jnp.concatenate(rest, axis=0).astype(jnp.bfloat16)

    for c in range(CHUNKS):
        if c > 0:
            load(c).wait()

        def forward(step, rest, c=c):
            slot = lax.rem(rest, count)
            if c == 0:
                load_first(slot).wait()
            project(psend, c, slot)
            if c == 0:

                @pl.when(step == 0)
                def _():
                    pl.semaphore_wait(barrier, count - 1 + places - 1 + 1)
                    for later in range(1, CHUNKS):
                        load(later).start()
                    for later in range(CHUNKS):
                        load_truth(later).start()

            send_preds(c, slot).start()
            return lax.div(rest, count)

        lax.fori_loop(0, count - 1, forward, sum(slot * count**k for k, slot in enumerate(ORDER)))
        if c == 0:
            load_first(0).wait()
        project(precv, c, 0)

    for copy in small[1:]:
        copy.wait()
    row = jnp.concatenate([var_in[...], jnp.zeros((1, LANES - nvar), jnp.float32)], axis=1)
    var[...] = jnp.broadcast_to(row, (LANES, LANES)).T

    total = jnp.zeros((8, LANES), jnp.float32)
    for c in range(CHUNKS):
        load_truth(c).wait()
        blocks_of(precv, c, 1, count, precv_sem.at[c]).wait()
        first = c * chunk // LANES + me * blocks

        def put(rows, values, c=c):
            grecv[c, 0, rows, :] = values[0].astype(jnp.bfloat16)
            for s in range(1, count):
                gsend[c, s, rows, :] = values[s].astype(jnp.bfloat16)

        def whole_rows(step, acc, c=c, first=first, put=put):
            block = lax.rem(step, blocks)
            lanes = pl.ds(pl.multiple_of(block * LANES, LANES), LANES)
            start = pl.multiple_of(lax.div(step, blocks) * ROWS, ROWS)
            rows = pl.ds(pl.multiple_of(block * whole + start, ROWS), ROWS)
            members = [precv[c, s, rows, :].astype(jnp.float32) for s in range(count)]
            target = truth[c, pl.ds(start, ROWS), lanes]
            scale = var[pl.ds(start, ROWS), :] * area[pl.ds(first + block, 1), :]
            terms, pulled = score_block(members, target, scale)
            put(rows, pulled)
            return acc + terms[:8] + terms[8:]

        total = lax.fori_loop(0, whole // ROWS * blocks, whole_rows, total)

        rows = pl.ds(tail, ROWS)
        members = [precv[c, s, rows, :].astype(jnp.float32)[:8] for s in range(count)]
        spare = [jnp.zeros((8 - blocks * left, LANES), jnp.float32)] if blocks * left < 8 else []
        target = jnp.concatenate(
            [truth[c, pl.ds(whole, left), pl.ds(b * LANES, LANES)] for b in range(blocks)] + spare, axis=0
        )
        scale = jnp.concatenate(
            [var[pl.ds(whole, left), :] * area[pl.ds(first + b, 1), :] for b in range(blocks)] + spare, axis=0
        )
        terms, pulled = score_block(members, target, scale)
        rest = jnp.zeros((ROWS - 8, LANES), jnp.float32)
        put(rows, [jnp.concatenate([value, rest], axis=0) for value in pulled])
        total = total + terms
        for slot in ORDER:
            send_grads(c, slot).start()
    partial = jnp.sum(total)

    cut = 256

    def weight_part(step, c, first=0, length=chunk):
        lanes = pl.ds(pl.multiple_of(step * cut, cut), cut)
        first = pl.multiple_of(first, LANES)
        part = jnp.dot(
            grads[:, pl.ds(first, length)],
            latent[pl.ds(pl.multiple_of(c * chunk + first, LANES), length), lanes],
            preferred_element_type=jnp.float32,
        )
        if c == 0:
            wsum[pl.ds(0, padded), lanes] = part
        else:
            wsum[pl.ds(0, padded), lanes] += part

    def latent_part(step, c):
        lanes = pl.ds(pl.multiple_of(step * cut, cut), cut)
        rows = pl.ds(pl.multiple_of(c * chunk + step * cut, cut), cut)
        out_ref[0, rows, :] = lax.dot_general(
            grads[:, lanes], weight[...], (((0,), (0,)), ((), ())), preferred_element_type=jnp.float32
        ).astype(jnp.bfloat16)

    def loop(start, stop, body):
        def step_of(step, carry):
            body(step)
            return carry

        lax.fori_loop(start, stop, step_of, 0)

    def unpack(slot, c):
        at = sent_to(slot) * width
        last = grecv[c, slot, pl.ds(tail, ROWS), :].astype(jnp.float32)
        for b in range(blocks):
            lanes = pl.ds(pl.multiple_of(at + b * LANES, LANES), LANES)
            grads[pl.ds(0, whole), lanes] = grecv[c, slot, pl.ds(b * whole, whole), :]
            grads[pl.ds(whole, ROWS), lanes] = jnp.concatenate(
                [last[b * left : (b + 1) * left], jnp.zeros((ROWS - left, LANES), jnp.float32)], axis=0
            ).astype(jnp.bfloat16)

    for c in range(CHUNKS - 1):
        blocks_of(grecv, c, half, count, grecv_sem.at[c, 1]).wait()
        blocks_of(grecv, c, 1, half, grecv_sem.at[c, 0]).wait()
        loop(0, count, lambda slot, c=c: unpack(slot, c))
        loop(0, lat // cut, lambda step, c=c: weight_part(step, c))
        loop(0, chunk // cut, lambda step, c=c: latent_part(step, c))

    c = CHUNKS - 1
    side = half * width
    blocks_of(grecv, c, 1, half, grecv_sem.at[c, 0]).wait()
    loop(0, half, lambda slot: unpack(slot, c))
    loop(0, lat // cut, lambda step: weight_part(step, c, my_y * side, side))
    blocks_of(grecv, c, half, count, grecv_sem.at[c, 1]).wait()
    loop(half, count, lambda slot: unpack(slot, c))

    wsum[pl.ds(padded, LANES - padded), :] = jnp.broadcast_to(partial, (LANES - padded, lat))

    def weight_sent(step):
        weight_part(step, c, (1 - my_y) * side, side)
        for b in range(cut // LANES):
            lanes = pl.ds(pl.multiple_of(step * cut + b * LANES, LANES), LANES)
            turned = wsum[:, lanes].T
            asend[0, step * 2 + b] = turned[: LANES // 2]
            asend[1, step * 2 + b] = turned[LANES // 2 :]
        send_core(step).start()

    loop(0, lat // cut, weight_sent)
    all_of(arecv, arecv_sem).wait()
    bsend[...] = asend[core] + arecv[...]
    for step in range(1, places):
        send_share(step).start()
    brecv[places - 1] = bsend[spot, pl.ds(pl.multiple_of(my_y * brecv.shape[1], 8), brecv.shape[1]), :]
    loop(0, chunk // cut, lambda step: latent_part(step, c))
    for c in range(CHUNKS):
        blocks_of(psend, c, 1, count, psend_sem.at[c]).wait()
        blocks_of(gsend, c, 1, count, gsend_sem.at[c]).wait()
    all_of(asend.at[1 - core], asend_sem).wait()
    all_of(brecv.at[pl.ds(0, places - 1)], brecv_sem).wait()

    def share_from(x, y):
        ways = (
            lax.rem(lax.rem(spot, 4) + 4 - x, 4),
            lax.rem(lax.div(spot, 4) * 2 + my_y + 4 - y, 4),
        )
        x, y = ((1 - lax.div(d, 2)) * (3 - 2 * d) + lax.div(d, 2) * (2 * d - 4) for d in ways)
        return brecv[x * 4 + y]

    summed = share_from(0, 0)
    for k in range(1, places):
        summed = summed + share_from(k // 4, k % 4)
    crecv[0] = summed
    for slot in range(1, count):
        send_sum(slot).start()
    all_of(brecv.at[pl.ds(0, places - 1)], bsend_sem).wait()
    all_of(crecv.at[pl.ds(1, count - 1)], crecv_sem).wait()
    for y in range(2):
        side_at = lax.rem(my_y + y, 2) * half
        final = crecv[side_at + my_z]
        for k in range(1, half):
            final = final + crecv[side_at + lax.rem(my_z + half - k, half)]
        summed_ref[pl.ds(y * brecv.shape[1], brecv.shape[1]), :] = final

    all_of(crecv.at[pl.ds(1, count - 1)], csend_sem).wait()


def copy_out(sizes, latent_grad, summed, latent_out, wgrad_out, loss_out, wgrad, loss, sem):
    count, shards, points, lat, nvar = sizes
    copies = [
        pltpu.make_async_copy(latent_grad, latent_out, sem.at[0]),
        pltpu.make_async_copy(wgrad, wgrad_out, sem.at[1]),
        pltpu.make_async_copy(loss, loss_out, sem.at[2]),
    ]
    copies[0].start()
    wgrad[...] = summed[:, :nvar] * (1.0 / math.sqrt(points * shards * count))
    loss[...] = summed[0:1, LANES - 1 : LANES] * (1.0 / (points * shards * nvar))
    for copy in copies[1:]:
        copy.start()
    for copy in copies:
        copy.wait()


def per_device(latent, proj_weight, truth, area_weight, var_weight):
    count, shards = lax.axis_size("ens"), lax.axis_size("grid")
    _, points, lat = latent.shape
    nvar = truth.shape[0]
    padded = -(-nvar // ROWS) * ROWS
    width = points // CHUNKS // count
    packed = width // LANES * (nvar // ROWS * ROWS) + ROWS
    share = lat // shards
    sizes = (count, shards, points, lat, nvar)
    hbm = pl.BlockSpec(memory_space=pltpu.HBM)
    vmem = pl.BlockSpec(memory_space=pltpu.VMEM)
    dma = pltpu.SemaphoreType.DMA
    out_shape = (
        jax.ShapeDtypeStruct((1, points, lat), jnp.bfloat16),
        jax.ShapeDtypeStruct((share, nvar), jnp.float32),
        jax.ShapeDtypeStruct((1, 1), jnp.float32),
    )
    latent_grad, summed = pl.pallas_call(
        functools.partial(kernel, sizes),
        out_shape=(pltpu.VMEM((1, points, lat), jnp.bfloat16), pltpu.VMEM((share, LANES), jnp.float32)),
        in_specs=[hbm] * 5,
        out_specs=(vmem, vmem),
        scratch_shapes=[
            pltpu.VMEM((points, lat), jnp.bfloat16),
            pltpu.VMEM((nvar, lat), jnp.bfloat16),
            pltpu.VMEM((padded, lat), jnp.bfloat16),
            pltpu.VMEM((CHUNKS, nvar, width), jnp.float32),
            pltpu.VMEM((points // LANES, LANES), jnp.float32),
            pltpu.VMEM((1, nvar), jnp.float32),
            pltpu.VMEM((LANES, LANES), jnp.float32),
            pltpu.VMEM((CHUNKS, count, packed, LANES), jnp.bfloat16),
            pltpu.VMEM((CHUNKS, count, packed, LANES), jnp.bfloat16),
            pltpu.VMEM((CHUNKS, count, packed, LANES), jnp.bfloat16),
            pltpu.VMEM((CHUNKS, count, packed, LANES), jnp.bfloat16),
            pltpu.VMEM((padded, points // CHUNKS), jnp.bfloat16),
            pltpu.VMEM((LANES, lat), jnp.float32),
            pltpu.VMEM((2, shards // 2, share, LANES), jnp.float32),
            pltpu.VMEM((shards // 2, share, LANES), jnp.float32),
            pltpu.VMEM((shards // 2, share, LANES), jnp.float32),
            pltpu.VMEM((shards, share // 2, LANES), jnp.float32),
            pltpu.VMEM((count, share // 2, LANES), jnp.float32),
            dma((CHUNKS,)),
            dma((count,)),
            dma((CHUNKS,)),
            dma((3,)),
            dma((CHUNKS,)),
            dma((CHUNKS,)),
            dma((CHUNKS,)),
            dma((CHUNKS, 2)),
            dma,
            dma,
            dma,
            dma,
            dma,
            dma,
        ],
        compiler_params=pltpu.CompilerParams(
            collective_id=0, has_side_effects=True, vmem_limit_bytes=36 * 2**20
        ),
        name="crps_step",
    )(
        *(
            pltpu.with_memory_space_constraint(x, pltpu.HBM)
            for x in (
                latent,
                proj_weight.T,
                truth,
                area_weight.reshape(points // LANES, LANES),
                var_weight.reshape(1, nvar),
            )
        )
    )
    latent_grad, weight_grad, loss = pl.pallas_call(
        functools.partial(copy_out, sizes),
        out_shape=out_shape,
        in_specs=[vmem, vmem],
        out_specs=(hbm, hbm, hbm),
        scratch_shapes=[
            pltpu.VMEM((share, nvar), jnp.float32),
            pltpu.VMEM((1, 1), jnp.float32),
            dma((3,)),
        ],
        compiler_params=pltpu.CompilerParams(vmem_limit_bytes=2**20),
        name="copy_out",
    )(*(pltpu.with_memory_space_constraint(x, pltpu.VMEM) for x in (latent_grad, summed)))
    return (loss[0, 0], latent_grad, weight_grad)


def solution(mesh):
    placed = (P("ens", "grid", None), P(), P(None, "grid"), P("grid"), P())
    return jax.shard_map(
        per_device,
        mesh=mesh,
        in_specs=placed,
        out_specs=(P(), P("ens", "grid", None), P("grid", None)),
        check_vma=False,
    )
```

```python
import functools
import math

import jax
import jax.numpy as jnp
from jax import lax
from jax.experimental import pallas as pl
from jax.experimental.pallas import tpu as pltpu
from jax.sharding import PartitionSpec as P

DELTA = 0.05
CHUNKS = 3
LANES = 128
ORDER = (3, 1, 2, 7, 5, 6, 4)
ROWS = 16
MESH = pl.DeviceIdType.MESH


def score_block(members, target, scale):
    count = len(members)
    square = DELTA * DELTA
    pulls = [None] * count
    spread = None
    for a in range(count):
        for b in range(a + 1, count):
            diff = members[a] - members[b]
            inner = diff * diff + square
            inverse = lax.rsqrt(inner)
            sign = diff * inverse
            root = inner * inverse
            spread = root if spread is None else spread + root
            pulls[a] = sign if pulls[a] is None else pulls[a] + sign
            pulls[b] = -sign if pulls[b] is None else pulls[b] - sign
    skill = None
    grads = []
    for a in range(count):
        diff = members[a] - target
        inner = diff * diff + square
        inverse = lax.rsqrt(inner)
        root = inner * inverse
        skill = root if skill is None else skill + root
        sign = diff * inverse
        grads.append(scale * (sign * (1.0 / count) - pulls[a] * (1.0 / (count * (count - 1)))))
    crps = skill * (1.0 / count) - spread * (1.0 / (count * (count - 1))) - 0.5 * DELTA
    return scale * crps, grads


def kernel(
    sizes,
    latent_hbm,
    weight_hbm,
    truth_hbm,
    area_hbm,
    var_hbm,
    out_ref,
    summed_ref,
    latent,
    weight_in,
    weight,
    truth,
    area,
    var_in,
    var,
    psend,
    precv,
    gsend,
    grecv,
    grads,
    wsum,
    asend,
    arecv,
    bsend,
    brecv,
    crecv,
    load_sem,
    first_sem,
    truth_sem,
    small_sem,
    psend_sem,
    precv_sem,
    gsend_sem,
    grecv_sem,
    asend_sem,
    arecv_sem,
    bsend_sem,
    brecv_sem,
    csend_sem,
    crecv_sem,
):
    count, shards, points, lat, nvar = sizes
    padded = weight.shape[0]
    chunk = points // CHUNKS
    width = chunk // count
    blocks = width // LANES
    half = count // 2
    whole = nvar // ROWS * ROWS
    left = nvar - whole
    tail = blocks * whole
    me = lax.axis_index("ens")
    mine = lax.axis_index("grid")
    my_y, my_z = lax.div(me, half), lax.rem(me, half)
    core, spot = lax.rem(mine, 2), lax.div(mine, 2)
    spots = shards // 2
    places = 2 * spots

    def member(slot, way):
        y, z = (slot // half, slot % half) if isinstance(slot, int) else (lax.div(slot, half), lax.rem(slot, half))
        return lax.rem(my_y + y, 2) * half + lax.rem(my_z + half + way * z, half)

    def sent_to(slot):
        return member(slot, 1)

    def came_from(slot):
        return member(slot, -1)

    def device_at(there):
        y, there = there
        return {"ens": y * half + my_z, "grid": there * 2 + core}

    def partner(step):
        far = (2, 1, 3, 0)
        x = lax.rem(lax.rem(spot, 4) + far[(step - 1) // 4], 4)
        y = lax.rem(lax.div(spot, 4) * 2 + my_y + far[(step - 1) % 4], 4)
        return lax.rem(y, 2), lax.div(y, 2) * 4 + x

    def load(c):
        rows = pl.ds(c * chunk, chunk)
        return pltpu.make_async_copy(latent_hbm.at[0, rows], latent.at[rows], load_sem.at[c])

    def load_first(slot):
        rows = pl.ds(pl.multiple_of(sent_to(slot) * width, LANES), width)
        return pltpu.make_async_copy(latent_hbm.at[0, rows], latent.at[rows], first_sem.at[slot])

    def load_truth(c):
        first = pl.multiple_of(c * chunk + me * width, LANES)
        return pltpu.make_async_copy(truth_hbm.at[:, pl.ds(first, width)], truth.at[c], truth_sem.at[c])

    sibling = mine + 1 - 2 * core
    barrier = pltpu.get_barrier_semaphore()
    for slot in range(1, count):
        pl.semaphore_signal(barrier, inc=1, device_id={"ens": sent_to(slot)}, device_id_type=MESH)
    for step in range(1, places):
        pl.semaphore_signal(barrier, inc=1, device_id=device_at(partner(step)), device_id_type=MESH)
    pl.semaphore_signal(barrier, inc=1, device_id={"grid": sibling}, device_id_type=MESH)

    small = [
        pltpu.make_async_copy(weight_hbm, weight_in, small_sem.at[0]),
        pltpu.make_async_copy(var_hbm, var_in, small_sem.at[1]),
        pltpu.make_async_copy(area_hbm, area, small_sem.at[2]),
    ]
    small[0].start()
    for slot in (*ORDER, 0):
        load_first(slot).start()
    for copy in small[1:]:
        copy.start()
    small[0].wait()
    weight[pl.ds(0, whole), :] = weight_in[pl.ds(0, whole), :]
    weight[pl.ds(whole, padded - whole), :] = jnp.concatenate(
        [
            weight_in[pl.ds(whole, left), :].astype(jnp.float32),
            jnp.zeros((padded - nvar, lat), jnp.float32),
        ],
        axis=0,
    ).astype(jnp.bfloat16)

    def send_preds(c, slot):
        return pltpu.make_async_remote_copy(
            src_ref=psend.at[c, slot],
            dst_ref=precv.at[c, slot],
            send_sem=psend_sem.at[c],
            recv_sem=precv_sem.at[c],
            device_id={"ens": sent_to(slot)},
            device_id_type=MESH,
        )

    def send_grads(c, slot):
        return pltpu.make_async_remote_copy(
            src_ref=gsend.at[c, slot],
            dst_ref=grecv.at[c, slot],
            send_sem=gsend_sem.at[c],
            recv_sem=grecv_sem.at[c, lax.div(slot, half) if not isinstance(slot, int) else slot // half],
            device_id={"ens": came_from(slot)},
            device_id_type=MESH,
        )

    def send_core(step):
        some = pl.ds(step * 2, 2)
        return pltpu.make_async_remote_copy(
            src_ref=asend.at[1 - core, some],
            dst_ref=arecv.at[some],
            send_sem=asend_sem,
            recv_sem=arecv_sem,
            device_id={"grid": sibling},
            device_id_type=MESH,
        )

    def send_share(step):
        y, there = partner(step)
        rows = pl.ds(pl.multiple_of(y * brecv.shape[1], 8), brecv.shape[1])
        return pltpu.make_async_remote_copy(
            src_ref=bsend.at[there, rows],
            dst_ref=brecv.at[step - 1],
            send_sem=bsend_sem,
            recv_sem=brecv_sem,
            device_id=device_at((y, there)),
            device_id_type=MESH,
        )

    def send_sum(slot):
        return pltpu.make_async_remote_copy(
            src_ref=crecv.at[0],
            dst_ref=crecv.at[slot],
            send_sem=csend_sem,
            recv_sem=crecv_sem,
            device_id={"ens": sent_to(slot)},
            device_id_type=MESH,
        )

    def all_of(some, sem):
        return pltpu.make_async_copy(some, some, sem)

    def blocks_of(ref, c, start, stop, sem):
        return all_of(ref.at[c, pl.ds(start, stop - start)], sem)

    def project(target, c, slot):
        first = pl.multiple_of(c * chunk + sent_to(slot) * width, LANES)
        preds = lax.dot_general(
            weight[...],
            latent[pl.ds(first, width), :],
            (((1,), (1,)), ((), ())),
            preferred_element_type=jnp.float32,
        )
        for b in range(blocks):
            target[c, slot, pl.ds(b * whole, whole), :] = preds[:whole, b * LANES : (b + 1) * LANES].astype(jnp.bfloat16)
        rest = [preds[whole:nvar, b * LANES : (b + 1) * LANES] for b in range(blocks)]
        rest.append(jnp.zeros((ROWS - blocks * left, LANES), jnp.float32))
        target[c, slot, pl.ds(tail, ROWS), :] = jnp.concatenate(rest, axis=0).astype(jnp.bfloat16)

    for c in range(CHUNKS):
        if c > 0:
            load(c).wait()

        def forward(step, rest, c=c):
            slot = lax.rem(rest, count)
            if c == 0:
                load_first(slot).wait()
            project(psend, c, slot)
            if c == 0:

                @pl.when(step == 0)
                def _():
                    pl.semaphore_wait(barrier, count - 1 + places - 1 + 1)
                    for later in range(1, CHUNKS):
                        load(later).start()
                    for later in range(CHUNKS):
                        load_truth(later).start()

            send_preds(c, slot).start()
            return lax.div(rest, count)

        lax.fori_loop(0, count - 1, forward, sum(slot * count**k for k, slot in enumerate(ORDER)))
        if c == 0:
            load_first(0).wait()
        project(precv, c, 0)

    for copy in small[1:]:
        copy.wait()
    row = jnp.concatenate([var_in[...], jnp.zeros((1, LANES - nvar), jnp.float32)], axis=1)
    var[...] = jnp.broadcast_to(row, (LANES, LANES)).T

    total = jnp.zeros((8, LANES), jnp.float32)
    for c in range(CHUNKS):
        load_truth(c).wait()
        blocks_of(precv, c, 1, count, precv_sem.at[c]).wait()
        first = c * chunk // LANES + me * blocks

        def put(rows, values, c=c):
            grecv[c, 0, rows, :] = values[0].astype(jnp.bfloat16)
            for s in range(1, count):
                gsend[c, s, rows, :] = values[s].astype(jnp.bfloat16)

        def whole_rows(step, acc, c=c, first=first, put=put):
            block = lax.rem(step, blocks)
            lanes = pl.ds(pl.multiple_of(block * LANES, LANES), LANES)
            start = pl.multiple_of(lax.div(step, blocks) * ROWS, ROWS)
            rows = pl.ds(pl.multiple_of(block * whole + start, ROWS), ROWS)
            members = [precv[c, s, rows, :].astype(jnp.float32) for s in range(count)]
            target = truth[c, pl.ds(start, ROWS), lanes]
            scale = var[pl.ds(start, ROWS), :] * area[pl.ds(first + block, 1), :]
            terms, pulled = score_block(members, target, scale)
            put(rows, pulled)
            return acc + terms[:8] + terms[8:]

        total = lax.fori_loop(0, whole // ROWS * blocks, whole_rows, total)

        rows = pl.ds(tail, ROWS)
        members = [precv[c, s, rows, :].astype(jnp.float32)[:8] for s in range(count)]
        spare = [jnp.zeros((8 - blocks * left, LANES), jnp.float32)] if blocks * left < 8 else []
        target = jnp.concatenate(
            [truth[c, pl.ds(whole, left), pl.ds(b * LANES, LANES)] for b in range(blocks)] + spare, axis=0
        )
        scale = jnp.concatenate(
            [var[pl.ds(whole, left), :] * area[pl.ds(first + b, 1), :] for b in range(blocks)] + spare, axis=0
        )
        terms, pulled = score_block(members, target, scale)
        rest = jnp.zeros((ROWS - 8, LANES), jnp.float32)
        put(rows, [jnp.concatenate([value, rest], axis=0) for value in pulled])
        total = total + terms
        for slot in ORDER:
            send_grads(c, slot).start()
    partial = jnp.sum(total)

    cut = 256

    def weight_part(step, c, first=0, length=chunk):
        lanes = pl.ds(pl.multiple_of(step * cut, cut), cut)
        first = pl.multiple_of(first, LANES)
        part = jnp.dot(
            grads[c, :, pl.ds(first, length)],
            latent[pl.ds(pl.multiple_of(c * chunk + first, LANES), length), lanes],
            preferred_element_type=jnp.float32,
        )
        if c == 0:
            wsum[pl.ds(0, padded), lanes] = part
        else:
            wsum[pl.ds(0, padded), lanes] += part

    def latent_part(step, c):
        lanes = pl.ds(pl.multiple_of(step * cut, cut), cut)
        rows = pl.ds(pl.multiple_of(c * chunk + step * cut, cut), cut)
        out_ref[0, rows, :] = lax.dot_general(
            grads[c, :, lanes], weight[...], (((0,), (0,)), ((), ())), preferred_element_type=jnp.float32
        ).astype(jnp.bfloat16)

    def loop(start, stop, body):
        def step_of(step, carry):
            body(step)
            return carry

        lax.fori_loop(start, stop, step_of, 0)

    def unpack(slot, c):
        at = sent_to(slot) * width
        last = grecv[c, slot, pl.ds(tail, ROWS), :].astype(jnp.float32)
        for b in range(blocks):
            lanes = pl.ds(pl.multiple_of(at + b * LANES, LANES), LANES)
            grads[c, pl.ds(0, whole), lanes] = grecv[c, slot, pl.ds(b * whole, whole), :]
            grads[c, pl.ds(whole, ROWS), lanes] = jnp.concatenate(
                [last[b * left : (b + 1) * left], jnp.zeros((ROWS - left, LANES), jnp.float32)], axis=0
            ).astype(jnp.bfloat16)

    for c in range(CHUNKS - 1):
        blocks_of(grecv, c, half, count, grecv_sem.at[c, 1]).wait()
        blocks_of(grecv, c, 1, half, grecv_sem.at[c, 0]).wait()
        loop(0, count, lambda slot, c=c: unpack(slot, c))
        loop(0, lat // cut, lambda step, c=c: weight_part(step, c))
        if c < CHUNKS - 2:
            loop(0, chunk // cut, lambda step, c=c: latent_part(step, c))

    c = CHUNKS - 1
    side = half * width
    blocks_of(grecv, c, 1, half, grecv_sem.at[c, 0]).wait()
    loop(0, half, lambda slot: unpack(slot, c))
    loop(0, lat // cut, lambda step: weight_part(step, c, my_y * side, side))
    blocks_of(grecv, c, half, count, grecv_sem.at[c, 1]).wait()
    loop(half, count, lambda slot: unpack(slot, c))

    wsum[pl.ds(padded, LANES - padded), :] = jnp.broadcast_to(partial, (LANES - padded, lat))

    def weight_sent(step):
        weight_part(step, c, (1 - my_y) * side, side)
        for b in range(cut // LANES):
            lanes = pl.ds(pl.multiple_of(step * cut + b * LANES, LANES), LANES)
            turned = wsum[:, lanes].T
            asend[0, step * 2 + b] = turned[: LANES // 2]
            asend[1, step * 2 + b] = turned[LANES // 2 :]
        send_core(step).start()

    loop(0, lat // cut, weight_sent)
    all_of(arecv, arecv_sem).wait()
    bsend[...] = asend[core] + arecv[...]
    for step in range(1, places):
        send_share(step).start()
    brecv[places - 1] = bsend[spot, pl.ds(pl.multiple_of(my_y * brecv.shape[1], 8), brecv.shape[1]), :]
    loop(0, chunk // cut, lambda step: latent_part(step, c))
    loop(0, 4, lambda step: latent_part(step, c - 1))
    for c in range(CHUNKS):
        blocks_of(psend, c, 1, count, psend_sem.at[c]).wait()
        blocks_of(gsend, c, 1, count, gsend_sem.at[c]).wait()
    all_of(asend.at[1 - core], asend_sem).wait()
    all_of(brecv.at[pl.ds(0, places - 1)], brecv_sem).wait()

    def share_from(x, y):
        ways = (
            lax.rem(lax.rem(spot, 4) + 4 - x, 4),
            lax.rem(lax.div(spot, 4) * 2 + my_y + 4 - y, 4),
        )
        x, y = ((1 - lax.div(d, 2)) * (3 - 2 * d) + lax.div(d, 2) * (2 * d - 4) for d in ways)
        return brecv[x * 4 + y]

    summed = share_from(0, 0)
    for k in range(1, places):
        summed = summed + share_from(k // 4, k % 4)
    crecv[0] = summed
    for slot in range(1, count):
        send_sum(slot).start()
    loop(4, chunk // cut, lambda step: latent_part(step, c - 1))
    all_of(brecv.at[pl.ds(0, places - 1)], bsend_sem).wait()
    all_of(crecv.at[pl.ds(1, count - 1)], crecv_sem).wait()
    for y in range(2):
        side_at = lax.rem(my_y + y, 2) * half
        final = crecv[side_at + my_z]
        for k in range(1, half):
            final = final + crecv[side_at + lax.rem(my_z + half - k, half)]
        summed_ref[pl.ds(y * brecv.shape[1], brecv.shape[1]), :] = final

    all_of(crecv.at[pl.ds(1, count - 1)], csend_sem).wait()


def copy_out(sizes, latent_grad, summed, latent_out, wgrad_out, loss_out, wgrad, loss, sem):
    count, shards, points, lat, nvar = sizes
    copies = [
        pltpu.make_async_copy(latent_grad, latent_out, sem.at[0]),
        pltpu.make_async_copy(wgrad, wgrad_out, sem.at[1]),
        pltpu.make_async_copy(loss, loss_out, sem.at[2]),
    ]
    copies[0].start()
    wgrad[...] = summed[:, :nvar] * (1.0 / math.sqrt(points * shards * count))
    loss[...] = summed[0:1, LANES - 1 : LANES] * (1.0 / (points * shards * nvar))
    for copy in copies[1:]:
        copy.start()
    for copy in copies:
        copy.wait()


def per_device(latent, proj_weight, truth, area_weight, var_weight):
    count, shards = lax.axis_size("ens"), lax.axis_size("grid")
    _, points, lat = latent.shape
    nvar = truth.shape[0]
    padded = -(-nvar // ROWS) * ROWS
    width = points // CHUNKS // count
    packed = width // LANES * (nvar // ROWS * ROWS) + ROWS
    share = lat // shards
    sizes = (count, shards, points, lat, nvar)
    hbm = pl.BlockSpec(memory_space=pltpu.HBM)
    vmem = pl.BlockSpec(memory_space=pltpu.VMEM)
    dma = pltpu.SemaphoreType.DMA
    out_shape = (
        jax.ShapeDtypeStruct((1, points, lat), jnp.bfloat16),
        jax.ShapeDtypeStruct((share, nvar), jnp.float32),
        jax.ShapeDtypeStruct((1, 1), jnp.float32),
    )
    latent_grad, summed = pl.pallas_call(
        functools.partial(kernel, sizes),
        out_shape=(pltpu.VMEM((1, points, lat), jnp.bfloat16), pltpu.VMEM((share, LANES), jnp.float32)),
        in_specs=[hbm] * 5,
        out_specs=(vmem, vmem),
        scratch_shapes=[
            pltpu.VMEM((points, lat), jnp.bfloat16),
            pltpu.VMEM((nvar, lat), jnp.bfloat16),
            pltpu.VMEM((padded, lat), jnp.bfloat16),
            pltpu.VMEM((CHUNKS, nvar, width), jnp.float32),
            pltpu.VMEM((points // LANES, LANES), jnp.float32),
            pltpu.VMEM((1, nvar), jnp.float32),
            pltpu.VMEM((LANES, LANES), jnp.float32),
            pltpu.VMEM((CHUNKS, count, packed, LANES), jnp.bfloat16),
            pltpu.VMEM((CHUNKS, count, packed, LANES), jnp.bfloat16),
            pltpu.VMEM((CHUNKS, count, packed, LANES), jnp.bfloat16),
            pltpu.VMEM((CHUNKS, count, packed, LANES), jnp.bfloat16),
            pltpu.VMEM((CHUNKS, padded, points // CHUNKS), jnp.bfloat16),
            pltpu.VMEM((LANES, lat), jnp.float32),
            pltpu.VMEM((2, shards // 2, share, LANES), jnp.float32),
            pltpu.VMEM((shards // 2, share, LANES), jnp.float32),
            pltpu.VMEM((shards // 2, share, LANES), jnp.float32),
            pltpu.VMEM((shards, share // 2, LANES), jnp.float32),
            pltpu.VMEM((count, share // 2, LANES), jnp.float32),
            dma((CHUNKS,)),
            dma((count,)),
            dma((CHUNKS,)),
            dma((3,)),
            dma((CHUNKS,)),
            dma((CHUNKS,)),
            dma((CHUNKS,)),
            dma((CHUNKS, 2)),
            dma,
            dma,
            dma,
            dma,
            dma,
            dma,
        ],
        compiler_params=pltpu.CompilerParams(
            collective_id=0, has_side_effects=True, vmem_limit_bytes=36 * 2**20
        ),
        name="crps_step",
    )(
        *(
            pltpu.with_memory_space_constraint(x, pltpu.HBM)
            for x in (
                latent,
                proj_weight.T,
                truth,
                area_weight.reshape(points // LANES, LANES),
                var_weight.reshape(1, nvar),
            )
        )
    )
    latent_grad, weight_grad, loss = pl.pallas_call(
        functools.partial(copy_out, sizes),
        out_shape=out_shape,
        in_specs=[vmem, vmem],
        out_specs=(hbm, hbm, hbm),
        scratch_shapes=[
            pltpu.VMEM((share, nvar), jnp.float32),
            pltpu.VMEM((1, 1), jnp.float32),
            dma((3,)),
        ],
        compiler_params=pltpu.CompilerParams(vmem_limit_bytes=2**20),
        name="copy_out",
    )(*(pltpu.with_memory_space_constraint(x, pltpu.VMEM) for x in (latent_grad, summed)))
    return (loss[0, 0], latent_grad, weight_grad)


def solution(mesh):
    placed = (P("ens", "grid", None), P(), P(None, "grid"), P("grid"), P())
    return jax.shard_map(
        per_device,
        mesh=mesh,
        in_specs=placed,
        out_specs=(P(), P("ens", "grid", None), P("grid", None)),
        check_vma=False,
    )
```

```python
import functools
import math

import jax
import jax.numpy as jnp
from jax import lax
from jax.experimental import pallas as pl
from jax.experimental.pallas import tpu as pltpu
from jax.sharding import PartitionSpec as P

DELTA = 0.05
CHUNKS = 3
LANES = 128
ORDER = (3, 1, 2, 7, 5, 6, 4)
ROWS = 16
MESH = pl.DeviceIdType.MESH


def score_block(members, target, scale):
    count = len(members)
    square = DELTA * DELTA
    pulls = [None] * count
    spread = None
    for a in range(count):
        for b in range(a + 1, count):
            diff = members[a] - members[b]
            inner = diff * diff + square
            inverse = lax.rsqrt(inner)
            sign = diff * inverse
            root = inner * inverse
            spread = root if spread is None else spread + root
            pulls[a] = sign if pulls[a] is None else pulls[a] + sign
            pulls[b] = -sign if pulls[b] is None else pulls[b] - sign
    skill = None
    grads = []
    for a in range(count):
        diff = members[a] - target
        inner = diff * diff + square
        inverse = lax.rsqrt(inner)
        root = inner * inverse
        skill = root if skill is None else skill + root
        sign = diff * inverse
        grads.append(scale * (sign * (1.0 / count) - pulls[a] * (1.0 / (count * (count - 1)))))
    crps = skill * (1.0 / count) - spread * (1.0 / (count * (count - 1))) - 0.5 * DELTA
    return scale * crps, grads


def kernel(
    sizes,
    latent_hbm,
    weight_hbm,
    truth_hbm,
    area_hbm,
    var_hbm,
    out_ref,
    summed_ref,
    latent,
    weight_in,
    weight,
    truth,
    area,
    var_in,
    var,
    psend,
    precv,
    gsend,
    grecv,
    grads,
    wsum,
    asend,
    arecv,
    bsend,
    brecv,
    crecv,
    load_sem,
    first_sem,
    truth_sem,
    small_sem,
    psend_sem,
    precv_sem,
    gsend_sem,
    grecv_sem,
    asend_sem,
    arecv_sem,
    bsend_sem,
    brecv_sem,
    csend_sem,
    crecv_sem,
):
    count, shards, points, lat, nvar = sizes
    padded = weight.shape[0]
    chunk = points // CHUNKS
    width = chunk // count
    blocks = width // LANES
    half = count // 2
    whole = nvar // ROWS * ROWS
    left = nvar - whole
    tail = blocks * whole
    me = lax.axis_index("ens")
    mine = lax.axis_index("grid")
    my_y, my_z = lax.div(me, half), lax.rem(me, half)
    core, spot = lax.rem(mine, 2), lax.div(mine, 2)
    spots = shards // 2
    places = 2 * spots

    def member(slot, way):
        y, z = (slot // half, slot % half) if isinstance(slot, int) else (lax.div(slot, half), lax.rem(slot, half))
        return lax.rem(my_y + y, 2) * half + lax.rem(my_z + half + way * z, half)

    def sent_to(slot):
        return member(slot, 1)

    def came_from(slot):
        return member(slot, -1)

    def device_at(there):
        y, there = there
        return {"ens": y * half + my_z, "grid": there * 2 + core}

    def partner(step):
        far = (2, 1, 3, 0)
        x = lax.rem(lax.rem(spot, 4) + far[(step - 1) // 4], 4)
        y = lax.rem(lax.div(spot, 4) * 2 + my_y + far[(step - 1) % 4], 4)
        return lax.rem(y, 2), lax.div(y, 2) * 4 + x

    def load(c):
        rows = pl.ds(c * chunk, chunk)
        return pltpu.make_async_copy(latent_hbm.at[0, rows], latent.at[rows], load_sem.at[c])

    def load_first(slot):
        rows = pl.ds(pl.multiple_of(sent_to(slot) * width, LANES), width)
        return pltpu.make_async_copy(latent_hbm.at[0, rows], latent.at[rows], first_sem.at[slot])

    def load_truth(c):
        first = pl.multiple_of(c * chunk + me * width, LANES)
        return pltpu.make_async_copy(truth_hbm.at[:, pl.ds(first, width)], truth.at[c], truth_sem.at[c])

    sibling = mine + 1 - 2 * core
    barrier = pltpu.get_barrier_semaphore()
    for slot in range(1, count):
        pl.semaphore_signal(barrier, inc=1, device_id={"ens": sent_to(slot)}, device_id_type=MESH)
    for step in range(1, places):
        pl.semaphore_signal(barrier, inc=1, device_id=device_at(partner(step)), device_id_type=MESH)
    pl.semaphore_signal(barrier, inc=1, device_id={"grid": sibling}, device_id_type=MESH)

    small = [
        pltpu.make_async_copy(weight_hbm, weight_in, small_sem.at[0]),
        pltpu.make_async_copy(var_hbm, var_in, small_sem.at[1]),
        pltpu.make_async_copy(area_hbm, area, small_sem.at[2]),
    ]
    small[0].start()
    for slot in (*ORDER, 0):
        load_first(slot).start()
    for copy in small[1:]:
        copy.start()
    small[0].wait()
    weight[pl.ds(0, whole), :] = weight_in[pl.ds(0, whole), :]
    weight[pl.ds(whole, padded - whole), :] = jnp.concatenate(
        [
            weight_in[pl.ds(whole, left), :].astype(jnp.float32),
            jnp.zeros((padded - nvar, lat), jnp.float32),
        ],
        axis=0,
    ).astype(jnp.bfloat16)

    def send_preds(c, slot):
        return pltpu.make_async_remote_copy(
            src_ref=psend.at[c, slot],
            dst_ref=precv.at[c, slot],
            send_sem=psend_sem.at[c],
            recv_sem=precv_sem.at[c],
            device_id={"ens": sent_to(slot)},
            device_id_type=MESH,
        )

    def send_grads(c, slot):
        return pltpu.make_async_remote_copy(
            src_ref=gsend.at[c, slot],
            dst_ref=grecv.at[c, slot],
            send_sem=gsend_sem.at[c],
            recv_sem=grecv_sem.at[c, lax.div(slot, half) if not isinstance(slot, int) else slot // half],
            device_id={"ens": came_from(slot)},
            device_id_type=MESH,
        )

    def send_core(step):
        some = pl.ds(step * 2, 2)
        return pltpu.make_async_remote_copy(
            src_ref=asend.at[1 - core, some],
            dst_ref=arecv.at[some],
            send_sem=asend_sem,
            recv_sem=arecv_sem,
            device_id={"grid": sibling},
            device_id_type=MESH,
        )

    def send_share(step):
        y, there = partner(step)
        rows = pl.ds(pl.multiple_of(y * brecv.shape[1], 8), brecv.shape[1])
        return pltpu.make_async_remote_copy(
            src_ref=bsend.at[there, rows],
            dst_ref=brecv.at[step - 1],
            send_sem=bsend_sem,
            recv_sem=brecv_sem,
            device_id=device_at((y, there)),
            device_id_type=MESH,
        )

    def send_sum(slot):
        return pltpu.make_async_remote_copy(
            src_ref=crecv.at[0],
            dst_ref=crecv.at[slot],
            send_sem=csend_sem,
            recv_sem=crecv_sem,
            device_id={"ens": sent_to(slot)},
            device_id_type=MESH,
        )

    def all_of(some, sem):
        return pltpu.make_async_copy(some, some, sem)

    def blocks_of(ref, c, start, stop, sem):
        return all_of(ref.at[c, pl.ds(start, stop - start)], sem)

    def project(target, c, slot):
        first = pl.multiple_of(c * chunk + sent_to(slot) * width, LANES)
        preds = lax.dot_general(
            weight[...],
            latent[pl.ds(first, width), :],
            (((1,), (1,)), ((), ())),
            preferred_element_type=jnp.float32,
        )
        for b in range(blocks):
            target[c, slot, pl.ds(b * whole, whole), :] = preds[:whole, b * LANES : (b + 1) * LANES].astype(jnp.bfloat16)
        rest = [preds[whole:nvar, b * LANES : (b + 1) * LANES] for b in range(blocks)]
        rest.append(jnp.zeros((ROWS - blocks * left, LANES), jnp.float32))
        target[c, slot, pl.ds(tail, ROWS), :] = jnp.concatenate(rest, axis=0).astype(jnp.bfloat16)

    for c in range(CHUNKS):
        if c > 0:
            load(c).wait()

        def forward(step, rest, c=c):
            slot = lax.rem(rest, count)
            if c == 0:
                load_first(slot).wait()
            project(psend, c, slot)
            if c == 0:

                @pl.when(step == 0)
                def _():
                    pl.semaphore_wait(barrier, count - 1 + places - 1 + 1)
                    for later in range(1, CHUNKS):
                        load(later).start()
                    for later in range(CHUNKS):
                        load_truth(later).start()

            send_preds(c, slot).start()
            return lax.div(rest, count)

        lax.fori_loop(0, count - 1, forward, sum(slot * count**k for k, slot in enumerate(ORDER)))
        if c == 0:
            load_first(0).wait()
        project(precv, c, 0)

    for copy in small[1:]:
        copy.wait()
    row = jnp.concatenate([var_in[...], jnp.zeros((1, LANES - nvar), jnp.float32)], axis=1)
    var[...] = jnp.broadcast_to(row, (LANES, LANES)).T

    total = jnp.zeros((8, LANES), jnp.float32)
    for c in range(CHUNKS):
        load_truth(c).wait()
        blocks_of(precv, c, 1, count, precv_sem.at[c]).wait()
        first = c * chunk // LANES + me * blocks

        def put(rows, values, c=c):
            grecv[c, 0, rows, :] = values[0].astype(jnp.bfloat16)
            for s in range(1, count):
                gsend[c, s, rows, :] = values[s].astype(jnp.bfloat16)

        def whole_rows(step, acc, c=c, first=first, put=put):
            block = lax.rem(step, blocks)
            lanes = pl.ds(pl.multiple_of(block * LANES, LANES), LANES)
            start = pl.multiple_of(lax.div(step, blocks) * ROWS, ROWS)
            rows = pl.ds(pl.multiple_of(block * whole + start, ROWS), ROWS)
            members = [precv[c, s, rows, :].astype(jnp.float32) for s in range(count)]
            target = truth[c, pl.ds(start, ROWS), lanes]
            scale = var[pl.ds(start, ROWS), :] * area[pl.ds(first + block, 1), :]
            terms, pulled = score_block(members, target, scale)
            put(rows, pulled)
            return acc + terms[:8] + terms[8:]

        total = lax.fori_loop(0, whole // ROWS * blocks, whole_rows, total)

        rows = pl.ds(tail, ROWS)
        members = [precv[c, s, rows, :].astype(jnp.float32)[:8] for s in range(count)]
        spare = [jnp.zeros((8 - blocks * left, LANES), jnp.float32)] if blocks * left < 8 else []
        target = jnp.concatenate(
            [truth[c, pl.ds(whole, left), pl.ds(b * LANES, LANES)] for b in range(blocks)] + spare, axis=0
        )
        scale = jnp.concatenate(
            [var[pl.ds(whole, left), :] * area[pl.ds(first + b, 1), :] for b in range(blocks)] + spare, axis=0
        )
        terms, pulled = score_block(members, target, scale)
        rest = jnp.zeros((ROWS - 8, LANES), jnp.float32)
        put(rows, [jnp.concatenate([value, rest], axis=0) for value in pulled])
        total = total + terms
        for slot in ORDER:
            send_grads(c, slot).start()
    partial = jnp.sum(total)

    cut = 256

    def weight_part(step, c, first=0, length=chunk):
        lanes = pl.ds(pl.multiple_of(step * cut, cut), cut)
        first = pl.multiple_of(first, LANES)
        part = jnp.dot(
            grads[c, :, pl.ds(first, length)],
            latent[pl.ds(pl.multiple_of(c * chunk + first, LANES), length), lanes],
            preferred_element_type=jnp.float32,
        )
        if c == 0:
            wsum[pl.ds(0, padded), lanes] = part
        else:
            wsum[pl.ds(0, padded), lanes] += part

    def latent_part(step, c):
        lanes = pl.ds(pl.multiple_of(step * cut, cut), cut)
        rows = pl.ds(pl.multiple_of(c * chunk + step * cut, cut), cut)
        out_ref[0, rows, :] = lax.dot_general(
            grads[c, :, lanes], weight[...], (((0,), (0,)), ((), ())), preferred_element_type=jnp.float32
        ).astype(jnp.bfloat16)

    def loop(start, stop, body):
        def step_of(step, carry):
            body(step)
            return carry

        lax.fori_loop(start, stop, step_of, 0)

    def unpack(slot, c):
        at = sent_to(slot) * width
        last = grecv[c, slot, pl.ds(tail, ROWS), :].astype(jnp.float32)
        for b in range(blocks):
            lanes = pl.ds(pl.multiple_of(at + b * LANES, LANES), LANES)
            grads[c, pl.ds(0, whole), lanes] = grecv[c, slot, pl.ds(b * whole, whole), :]
            grads[c, pl.ds(whole, ROWS), lanes] = jnp.concatenate(
                [last[b * left : (b + 1) * left], jnp.zeros((ROWS - left, LANES), jnp.float32)], axis=0
            ).astype(jnp.bfloat16)

    for c in range(CHUNKS - 1):
        blocks_of(grecv, c, half, count, grecv_sem.at[c, 1]).wait()
        blocks_of(grecv, c, 1, half, grecv_sem.at[c, 0]).wait()
        loop(0, count, lambda slot, c=c: unpack(slot, c))
        loop(0, lat // cut, lambda step, c=c: weight_part(step, c))
        if c < CHUNKS - 2:
            loop(0, chunk // cut, lambda step, c=c: latent_part(step, c))

    c = CHUNKS - 1
    side = half * width
    blocks_of(grecv, c, 1, half, grecv_sem.at[c, 0]).wait()
    loop(0, half, lambda slot: unpack(slot, c))
    loop(0, lat // cut, lambda step: weight_part(step, c, my_y * side, side))
    blocks_of(grecv, c, half, count, grecv_sem.at[c, 1]).wait()
    loop(half, count, lambda slot: unpack(slot, c))

    wsum[pl.ds(padded, LANES - padded), :] = jnp.broadcast_to(partial, (LANES - padded, lat))

    def weight_sent(step):
        weight_part(step, c, (1 - my_y) * side, side)
        for b in range(cut // LANES):
            lanes = pl.ds(pl.multiple_of(step * cut + b * LANES, LANES), LANES)
            turned = wsum[:, lanes].T
            asend[0, step * 2 + b] = turned[: LANES // 2]
            asend[1, step * 2 + b] = turned[LANES // 2 :]
        send_core(step).start()

    loop(0, lat // cut, weight_sent)
    all_of(arecv, arecv_sem).wait()
    bsend[...] = asend[core] + arecv[...]
    for step in range(1, places):
        send_share(step).start()
    brecv[places - 1] = bsend[spot, pl.ds(pl.multiple_of(my_y * brecv.shape[1], 8), brecv.shape[1]), :]
    loop(0, chunk // cut, lambda step: latent_part(step, c))
    loop(0, 4, lambda step: latent_part(step, c - 1))
    for c in range(CHUNKS):
        blocks_of(psend, c, 1, count, psend_sem.at[c]).wait()
        blocks_of(gsend, c, 1, count, gsend_sem.at[c]).wait()
    all_of(asend.at[1 - core], asend_sem).wait()
    all_of(brecv.at[pl.ds(0, places - 1)], brecv_sem).wait()

    def share_from(x, y):
        ways = (
            lax.rem(lax.rem(spot, 4) + 4 - x, 4),
            lax.rem(lax.div(spot, 4) * 2 + my_y + 4 - y, 4),
        )
        x, y = ((1 - lax.div(d, 2)) * (3 - 2 * d) + lax.div(d, 2) * (2 * d - 4) for d in ways)
        return brecv[x * 4 + y]

    summed = share_from(0, 0)
    for k in range(1, places):
        summed = summed + share_from(k // 4, k % 4)
    crecv[0] = summed
    for slot in (6, 5, 7, 2, 4, 1, 3):
        send_sum(slot).start()
    loop(4, chunk // cut, lambda step: latent_part(step, c - 1))
    all_of(brecv.at[pl.ds(0, places - 1)], bsend_sem).wait()
    all_of(crecv.at[pl.ds(1, count - 1)], crecv_sem).wait()
    for y in range(2):
        side_at = lax.rem(my_y + y, 2) * half
        final = crecv[side_at + my_z]
        for k in range(1, half):
            final = final + crecv[side_at + lax.rem(my_z + half - k, half)]
        summed_ref[pl.ds(y * brecv.shape[1], brecv.shape[1]), :] = final

    all_of(crecv.at[pl.ds(1, count - 1)], csend_sem).wait()


def copy_out(sizes, latent_grad, summed, latent_out, wgrad_out, loss_out, wgrad, loss, sem):
    count, shards, points, lat, nvar = sizes
    copies = [
        pltpu.make_async_copy(latent_grad, latent_out, sem.at[0]),
        pltpu.make_async_copy(wgrad, wgrad_out, sem.at[1]),
        pltpu.make_async_copy(loss, loss_out, sem.at[2]),
    ]
    copies[0].start()
    wgrad[...] = summed[:, :nvar] * (1.0 / math.sqrt(points * shards * count))
    loss[...] = summed[0:1, LANES - 1 : LANES] * (1.0 / (points * shards * nvar))
    for copy in copies[1:]:
        copy.start()
    for copy in copies:
        copy.wait()


def per_device(latent, proj_weight, truth, area_weight, var_weight):
    count, shards = lax.axis_size("ens"), lax.axis_size("grid")
    _, points, lat = latent.shape
    nvar = truth.shape[0]
    padded = -(-nvar // ROWS) * ROWS
    width = points // CHUNKS // count
    packed = width // LANES * (nvar // ROWS * ROWS) + ROWS
    share = lat // shards
    sizes = (count, shards, points, lat, nvar)
    hbm = pl.BlockSpec(memory_space=pltpu.HBM)
    vmem = pl.BlockSpec(memory_space=pltpu.VMEM)
    dma = pltpu.SemaphoreType.DMA
    out_shape = (
        jax.ShapeDtypeStruct((1, points, lat), jnp.bfloat16),
        jax.ShapeDtypeStruct((share, nvar), jnp.float32),
        jax.ShapeDtypeStruct((1, 1), jnp.float32),
    )
    latent_grad, summed = pl.pallas_call(
        functools.partial(kernel, sizes),
        out_shape=(pltpu.VMEM((1, points, lat), jnp.bfloat16), pltpu.VMEM((share, LANES), jnp.float32)),
        in_specs=[hbm] * 5,
        out_specs=(vmem, vmem),
        scratch_shapes=[
            pltpu.VMEM((points, lat), jnp.bfloat16),
            pltpu.VMEM((nvar, lat), jnp.bfloat16),
            pltpu.VMEM((padded, lat), jnp.bfloat16),
            pltpu.VMEM((CHUNKS, nvar, width), jnp.float32),
            pltpu.VMEM((points // LANES, LANES), jnp.float32),
            pltpu.VMEM((1, nvar), jnp.float32),
            pltpu.VMEM((LANES, LANES), jnp.float32),
            pltpu.VMEM((CHUNKS, count, packed, LANES), jnp.bfloat16),
            pltpu.VMEM((CHUNKS, count, packed, LANES), jnp.bfloat16),
            pltpu.VMEM((CHUNKS, count, packed, LANES), jnp.bfloat16),
            pltpu.VMEM((CHUNKS, count, packed, LANES), jnp.bfloat16),
            pltpu.VMEM((CHUNKS, padded, points // CHUNKS), jnp.bfloat16),
            pltpu.VMEM((LANES, lat), jnp.float32),
            pltpu.VMEM((2, shards // 2, share, LANES), jnp.float32),
            pltpu.VMEM((shards // 2, share, LANES), jnp.float32),
            pltpu.VMEM((shards // 2, share, LANES), jnp.float32),
            pltpu.VMEM((shards, share // 2, LANES), jnp.float32),
            pltpu.VMEM((count, share // 2, LANES), jnp.float32),
            dma((CHUNKS,)),
            dma((count,)),
            dma((CHUNKS,)),
            dma((3,)),
            dma((CHUNKS,)),
            dma((CHUNKS,)),
            dma((CHUNKS,)),
            dma((CHUNKS, 2)),
            dma,
            dma,
            dma,
            dma,
            dma,
            dma,
        ],
        compiler_params=pltpu.CompilerParams(
            collective_id=0, has_side_effects=True, vmem_limit_bytes=36 * 2**20
        ),
        name="crps_step",
    )(
        *(
            pltpu.with_memory_space_constraint(x, pltpu.HBM)
            for x in (
                latent,
                proj_weight.T,
                truth,
                area_weight.reshape(points // LANES, LANES),
                var_weight.reshape(1, nvar),
            )
        )
    )
    latent_grad, weight_grad, loss = pl.pallas_call(
        functools.partial(copy_out, sizes),
        out_shape=out_shape,
        in_specs=[vmem, vmem],
        out_specs=(hbm, hbm, hbm),
        scratch_shapes=[
            pltpu.VMEM((share, nvar), jnp.float32),
            pltpu.VMEM((1, 1), jnp.float32),
            dma((3,)),
        ],
        compiler_params=pltpu.CompilerParams(vmem_limit_bytes=2**20),
        name="copy_out",
    )(*(pltpu.with_memory_space_constraint(x, pltpu.VMEM) for x in (latent_grad, summed)))
    return (loss[0, 0], latent_grad, weight_grad)


def solution(mesh):
    placed = (P("ens", "grid", None), P(), P(None, "grid"), P("grid"), P())
    return jax.shard_map(
        per_device,
        mesh=mesh,
        in_specs=placed,
        out_specs=(P(), P("ens", "grid", None), P("grid", None)),
        check_vma=False,
    )
```

```python
import functools
import math

import jax
import jax.numpy as jnp
from jax import lax
from jax.experimental import pallas as pl
from jax.experimental.pallas import tpu as pltpu
from jax.sharding import PartitionSpec as P

DELTA = 0.05
CHUNKS = 3
LANES = 128
ORDER = (3, 1, 2, 7, 5, 6, 4)
ROWS = 16
MESH = pl.DeviceIdType.MESH


def score_block(members, target, scale):
    count = len(members)
    square = DELTA * DELTA
    pulls = [None] * count
    spread = None
    for a in range(count):
        for b in range(a + 1, count):
            diff = members[a] - members[b]
            inner = diff * diff + square
            inverse = lax.rsqrt(inner)
            sign = diff * inverse
            root = inner * inverse
            spread = root if spread is None else spread + root
            pulls[a] = sign if pulls[a] is None else pulls[a] + sign
            pulls[b] = -sign if pulls[b] is None else pulls[b] - sign
    skill = None
    grads = []
    for a in range(count):
        diff = members[a] - target
        inner = diff * diff + square
        inverse = lax.rsqrt(inner)
        root = inner * inverse
        skill = root if skill is None else skill + root
        sign = diff * inverse
        grads.append(scale * (sign * (1.0 / count) - pulls[a] * (1.0 / (count * (count - 1)))))
    crps = skill * (1.0 / count) - spread * (1.0 / (count * (count - 1))) - 0.5 * DELTA
    return scale * crps, grads


def kernel(
    sizes,
    latent_hbm,
    weight_hbm,
    truth_hbm,
    area_hbm,
    var_hbm,
    out_ref,
    summed_ref,
    latent,
    weight_in,
    weight,
    truth,
    area,
    var_in,
    var,
    psend,
    precv,
    gsend,
    grecv,
    grads,
    wsum,
    asend,
    arecv,
    bsend,
    brecv,
    crecv,
    load_sem,
    first_sem,
    truth_sem,
    small_sem,
    psend_sem,
    precv_sem,
    gsend_sem,
    grecv_sem,
    asend_sem,
    arecv_sem,
    bsend_sem,
    brecv_sem,
    csend_sem,
    crecv_sem,
):
    count, shards, points, lat, nvar = sizes
    padded = weight.shape[0]
    chunk = points // CHUNKS
    width = chunk // count
    blocks = width // LANES
    half = count // 2
    whole = nvar // ROWS * ROWS
    left = nvar - whole
    tail = blocks * whole
    me = lax.axis_index("ens")
    mine = lax.axis_index("grid")
    my_y, my_z = lax.div(me, half), lax.rem(me, half)
    core, spot = lax.rem(mine, 2), lax.div(mine, 2)
    spots = shards // 2
    places = 2 * spots

    def member(slot, way):
        y, z = (slot // half, slot % half) if isinstance(slot, int) else (lax.div(slot, half), lax.rem(slot, half))
        return lax.rem(my_y + y, 2) * half + lax.rem(my_z + half + way * z, half)

    def sent_to(slot):
        return member(slot, 1)

    def came_from(slot):
        return member(slot, -1)

    def device_at(there):
        y, there = there
        return {"ens": y * half + my_z, "grid": there * 2 + core}

    def partner(step):
        far = (2, 1, 3, 0)
        x = lax.rem(lax.rem(spot, 4) + far[(step - 1) // 4], 4)
        y = lax.rem(lax.div(spot, 4) * 2 + my_y + far[(step - 1) % 4], 4)
        return lax.rem(y, 2), lax.div(y, 2) * 4 + x

    def load(c):
        rows = pl.ds(c * chunk, chunk)
        return pltpu.make_async_copy(latent_hbm.at[0, rows], latent.at[rows], load_sem.at[c])

    def load_first(slot):
        rows = pl.ds(pl.multiple_of(sent_to(slot) * width, LANES), width)
        return pltpu.make_async_copy(latent_hbm.at[0, rows], latent.at[rows], first_sem.at[slot])

    def load_truth(c):
        first = pl.multiple_of(c * chunk + me * width, LANES)
        return pltpu.make_async_copy(truth_hbm.at[:, pl.ds(first, width)], truth.at[c], truth_sem.at[c])

    sibling = mine + 1 - 2 * core
    barrier = pltpu.get_barrier_semaphore()
    for slot in range(1, count):
        pl.semaphore_signal(barrier, inc=1, device_id={"ens": sent_to(slot)}, device_id_type=MESH)
    for step in range(1, places):
        pl.semaphore_signal(barrier, inc=1, device_id=device_at(partner(step)), device_id_type=MESH)
    pl.semaphore_signal(barrier, inc=1, device_id={"grid": sibling}, device_id_type=MESH)

    small = [
        pltpu.make_async_copy(weight_hbm, weight_in, small_sem.at[0]),
        pltpu.make_async_copy(var_hbm, var_in, small_sem.at[1]),
        pltpu.make_async_copy(area_hbm, area, small_sem.at[2]),
    ]
    small[0].start()
    for slot in (*ORDER, 0):
        load_first(slot).start()
    for copy in small[1:]:
        copy.start()
    small[0].wait()
    weight[pl.ds(0, whole), :] = weight_in[pl.ds(0, whole), :]
    weight[pl.ds(whole, padded - whole), :] = jnp.concatenate(
        [
            weight_in[pl.ds(whole, left), :].astype(jnp.float32),
            jnp.zeros((padded - nvar, lat), jnp.float32),
        ],
        axis=0,
    ).astype(jnp.bfloat16)

    def send_preds(c, slot):
        return pltpu.make_async_remote_copy(
            src_ref=psend.at[c, slot],
            dst_ref=precv.at[c, slot],
            send_sem=psend_sem.at[c],
            recv_sem=precv_sem.at[c],
            device_id={"ens": sent_to(slot)},
            device_id_type=MESH,
        )

    def send_grads(c, slot):
        return pltpu.make_async_remote_copy(
            src_ref=gsend.at[c, slot],
            dst_ref=grecv.at[c, slot],
            send_sem=gsend_sem.at[c],
            recv_sem=grecv_sem.at[c, lax.div(slot, half) if not isinstance(slot, int) else slot // half],
            device_id={"ens": came_from(slot)},
            device_id_type=MESH,
        )

    def send_core(step):
        some = pl.ds(step * 2, 2)
        return pltpu.make_async_remote_copy(
            src_ref=asend.at[1 - core, some],
            dst_ref=arecv.at[some],
            send_sem=asend_sem,
            recv_sem=arecv_sem,
            device_id={"grid": sibling},
            device_id_type=MESH,
        )

    def send_share(step):
        y, there = partner(step)
        rows = pl.ds(pl.multiple_of(y * brecv.shape[1], 8), brecv.shape[1])
        return pltpu.make_async_remote_copy(
            src_ref=bsend.at[there, rows],
            dst_ref=brecv.at[step - 1],
            send_sem=bsend_sem,
            recv_sem=brecv_sem,
            device_id=device_at((y, there)),
            device_id_type=MESH,
        )

    def send_sum(slot):
        return pltpu.make_async_remote_copy(
            src_ref=crecv.at[0],
            dst_ref=crecv.at[slot],
            send_sem=csend_sem,
            recv_sem=crecv_sem,
            device_id={"ens": sent_to(slot)},
            device_id_type=MESH,
        )

    def all_of(some, sem):
        return pltpu.make_async_copy(some, some, sem)

    def blocks_of(ref, c, start, stop, sem):
        return all_of(ref.at[c, pl.ds(start, stop - start)], sem)

    def project(target, c, slot):
        first = pl.multiple_of(c * chunk + sent_to(slot) * width, LANES)
        preds = lax.dot_general(
            weight[...],
            latent[pl.ds(first, width), :],
            (((1,), (1,)), ((), ())),
            preferred_element_type=jnp.float32,
        )
        for b in range(blocks):
            target[c, slot, pl.ds(b * whole, whole), :] = preds[:whole, b * LANES : (b + 1) * LANES].astype(jnp.bfloat16)
        rest = [preds[whole:nvar, b * LANES : (b + 1) * LANES] for b in range(blocks)]
        rest.append(jnp.zeros((ROWS - blocks * left, LANES), jnp.float32))
        target[c, slot, pl.ds(tail, ROWS), :] = jnp.concatenate(rest, axis=0).astype(jnp.bfloat16)

    for c in range(CHUNKS):
        if c > 0:
            load(c).wait()

        def forward(step, rest, c=c):
            slot = lax.rem(rest, count)
            if c == 0:
                load_first(slot).wait()
            project(psend, c, slot)
            if c == 0:

                @pl.when(step == 0)
                def _():
                    pl.semaphore_wait(barrier, count - 1 + places - 1 + 1)
                    for later in range(1, CHUNKS):
                        load(later).start()
                    for later in range(CHUNKS):
                        load_truth(later).start()

            send_preds(c, slot).start()
            return lax.div(rest, count)

        lax.fori_loop(0, count - 1, forward, sum(slot * count**k for k, slot in enumerate(ORDER)))
        if c == 0:
            load_first(0).wait()
        project(precv, c, 0)

    for copy in small[1:]:
        copy.wait()
    row = jnp.concatenate([var_in[...], jnp.zeros((1, LANES - nvar), jnp.float32)], axis=1)
    var[...] = jnp.broadcast_to(row, (LANES, LANES)).T

    total = jnp.zeros((8, LANES), jnp.float32)
    for c in range(CHUNKS):
        load_truth(c).wait()
        blocks_of(precv, c, 1, count, precv_sem.at[c]).wait()
        first = c * chunk // LANES + me * blocks

        def put(rows, values, c=c):
            grecv[c, 0, rows, :] = values[0].astype(jnp.bfloat16)
            for s in range(1, count):
                gsend[c, s, rows, :] = values[s].astype(jnp.bfloat16)

        def whole_rows(step, acc, c=c, first=first, put=put):
            block = lax.rem(step, blocks)
            lanes = pl.ds(pl.multiple_of(block * LANES, LANES), LANES)
            start = pl.multiple_of(lax.div(step, blocks) * ROWS, ROWS)
            rows = pl.ds(pl.multiple_of(block * whole + start, ROWS), ROWS)
            members = [precv[c, s, rows, :].astype(jnp.float32) for s in range(count)]
            target = truth[c, pl.ds(start, ROWS), lanes]
            scale = var[pl.ds(start, ROWS), :] * area[pl.ds(first + block, 1), :]
            terms, pulled = score_block(members, target, scale)
            put(rows, pulled)
            return acc + terms[:8] + terms[8:]

        total = lax.fori_loop(0, whole // ROWS * blocks, whole_rows, total)

        rows = pl.ds(tail, ROWS)
        members = [precv[c, s, rows, :].astype(jnp.float32)[:8] for s in range(count)]
        spare = [jnp.zeros((8 - blocks * left, LANES), jnp.float32)] if blocks * left < 8 else []
        target = jnp.concatenate(
            [truth[c, pl.ds(whole, left), pl.ds(b * LANES, LANES)] for b in range(blocks)] + spare, axis=0
        )
        scale = jnp.concatenate(
            [var[pl.ds(whole, left), :] * area[pl.ds(first + b, 1), :] for b in range(blocks)] + spare, axis=0
        )
        terms, pulled = score_block(members, target, scale)
        rest = jnp.zeros((ROWS - 8, LANES), jnp.float32)
        put(rows, [jnp.concatenate([value, rest], axis=0) for value in pulled])
        total = total + terms
        for slot in ORDER:
            send_grads(c, slot).start()
    partial = jnp.sum(total)

    cut = 256

    def weight_part(step, c, first=0, length=chunk):
        lanes = pl.ds(pl.multiple_of(step * cut, cut), cut)
        first = pl.multiple_of(first, LANES)
        part = jnp.dot(
            grads[c, :, pl.ds(first, length)],
            latent[pl.ds(pl.multiple_of(c * chunk + first, LANES), length), lanes],
            preferred_element_type=jnp.float32,
        )
        if c == 0:
            wsum[pl.ds(0, padded), lanes] = part
        else:
            wsum[pl.ds(0, padded), lanes] += part

    def latent_part(step, c):
        lanes = pl.ds(pl.multiple_of(step * cut, cut), cut)
        rows = pl.ds(pl.multiple_of(c * chunk + step * cut, cut), cut)
        out_ref[0, rows, :] = lax.dot_general(
            grads[c, :, lanes], weight[...], (((0,), (0,)), ((), ())), preferred_element_type=jnp.float32
        ).astype(jnp.bfloat16)

    def loop(start, stop, body):
        def step_of(step, carry):
            body(step)
            return carry

        lax.fori_loop(start, stop, step_of, 0)

    def unpack(slot, c):
        at = sent_to(slot) * width
        last = grecv[c, slot, pl.ds(tail, ROWS), :].astype(jnp.float32)
        for b in range(blocks):
            lanes = pl.ds(pl.multiple_of(at + b * LANES, LANES), LANES)
            grads[c, pl.ds(0, whole), lanes] = grecv[c, slot, pl.ds(b * whole, whole), :]
            grads[c, pl.ds(whole, ROWS), lanes] = jnp.concatenate(
                [last[b * left : (b + 1) * left], jnp.zeros((ROWS - left, LANES), jnp.float32)], axis=0
            ).astype(jnp.bfloat16)

    for c in range(CHUNKS - 1):
        blocks_of(grecv, c, half, count, grecv_sem.at[c, 1]).wait()
        blocks_of(grecv, c, 1, half, grecv_sem.at[c, 0]).wait()
        loop(0, count, lambda slot, c=c: unpack(slot, c))
        loop(0, lat // cut, lambda step, c=c: weight_part(step, c))
        if c < CHUNKS - 2:
            loop(0, chunk // cut, lambda step, c=c: latent_part(step, c))

    c = CHUNKS - 1
    side = half * width
    blocks_of(grecv, c, 1, half, grecv_sem.at[c, 0]).wait()
    loop(0, half, lambda slot: unpack(slot, c))
    loop(0, lat // cut, lambda step: weight_part(step, c, my_y * side, side))
    blocks_of(grecv, c, half, count, grecv_sem.at[c, 1]).wait()
    loop(half, count, lambda slot: unpack(slot, c))

    wsum[pl.ds(padded, LANES - padded), :] = jnp.broadcast_to(partial, (LANES - padded, lat))

    def weight_sent(step):
        lanes = pl.ds(pl.multiple_of(step * cut, cut), cut)
        first = pl.multiple_of((1 - my_y) * side, LANES)
        part = jnp.dot(
            grads[c, :, pl.ds(first, side)],
            latent[pl.ds(pl.multiple_of(c * chunk + first, LANES), side), lanes],
            preferred_element_type=jnp.float32,
        )
        part = jnp.concatenate([wsum[pl.ds(0, padded), lanes] + part, wsum[pl.ds(padded, LANES - padded), lanes]], axis=0)
        for b in range(cut // LANES):
            turned = part[:, b * LANES : (b + 1) * LANES].T
            asend[0, step * 2 + b] = turned[: LANES // 2]
            asend[1, step * 2 + b] = turned[LANES // 2 :]
        send_core(step).start()

    loop(0, lat // cut, weight_sent)
    all_of(arecv, arecv_sem).wait()
    bsend[...] = asend[core] + arecv[...]
    for step in range(1, places):
        send_share(step).start()
    brecv[places - 1] = bsend[spot, pl.ds(pl.multiple_of(my_y * brecv.shape[1], 8), brecv.shape[1]), :]
    loop(0, chunk // cut, lambda step: latent_part(step, c))
    loop(0, 4, lambda step: latent_part(step, c - 1))
    for c in range(CHUNKS):
        blocks_of(psend, c, 1, count, psend_sem.at[c]).wait()
        blocks_of(gsend, c, 1, count, gsend_sem.at[c]).wait()
    all_of(asend.at[1 - core], asend_sem).wait()
    all_of(brecv.at[pl.ds(0, places - 1)], brecv_sem).wait()

    def share_from(x, y):
        ways = (
            lax.rem(lax.rem(spot, 4) + 4 - x, 4),
            lax.rem(lax.div(spot, 4) * 2 + my_y + 4 - y, 4),
        )
        x, y = ((1 - lax.div(d, 2)) * (3 - 2 * d) + lax.div(d, 2) * (2 * d - 4) for d in ways)
        return brecv[x * 4 + y]

    summed = share_from(0, 0)
    for k in range(1, places):
        summed = summed + share_from(k // 4, k % 4)
    crecv[0] = summed
    for slot in range(1, count):
        send_sum(slot).start()
    loop(4, chunk // cut, lambda step: latent_part(step, c - 1))
    all_of(brecv.at[pl.ds(0, places - 1)], bsend_sem).wait()
    all_of(crecv.at[pl.ds(1, count - 1)], crecv_sem).wait()
    for y in range(2):
        side_at = lax.rem(my_y + y, 2) * half
        final = crecv[side_at + my_z]
        for k in range(1, half):
            final = final + crecv[side_at + lax.rem(my_z + half - k, half)]
        summed_ref[pl.ds(y * brecv.shape[1], brecv.shape[1]), :] = final

    all_of(crecv.at[pl.ds(1, count - 1)], csend_sem).wait()


def copy_out(sizes, latent_grad, summed, latent_out, wgrad_out, loss_out, wgrad, loss, sem):
    count, shards, points, lat, nvar = sizes
    copies = [
        pltpu.make_async_copy(latent_grad, latent_out, sem.at[0]),
        pltpu.make_async_copy(wgrad, wgrad_out, sem.at[1]),
        pltpu.make_async_copy(loss, loss_out, sem.at[2]),
    ]
    copies[0].start()
    wgrad[...] = summed[:, :nvar] * (1.0 / math.sqrt(points * shards * count))
    loss[...] = summed[0:1, LANES - 1 : LANES] * (1.0 / (points * shards * nvar))
    for copy in copies[1:]:
        copy.start()
    for copy in copies:
        copy.wait()


def per_device(latent, proj_weight, truth, area_weight, var_weight):
    count, shards = lax.axis_size("ens"), lax.axis_size("grid")
    _, points, lat = latent.shape
    nvar = truth.shape[0]
    padded = -(-nvar // ROWS) * ROWS
    width = points // CHUNKS // count
    packed = width // LANES * (nvar // ROWS * ROWS) + ROWS
    share = lat // shards
    sizes = (count, shards, points, lat, nvar)
    hbm = pl.BlockSpec(memory_space=pltpu.HBM)
    vmem = pl.BlockSpec(memory_space=pltpu.VMEM)
    dma = pltpu.SemaphoreType.DMA
    out_shape = (
        jax.ShapeDtypeStruct((1, points, lat), jnp.bfloat16),
        jax.ShapeDtypeStruct((share, nvar), jnp.float32),
        jax.ShapeDtypeStruct((1, 1), jnp.float32),
    )
    latent_grad, summed = pl.pallas_call(
        functools.partial(kernel, sizes),
        out_shape=(pltpu.VMEM((1, points, lat), jnp.bfloat16), pltpu.VMEM((share, LANES), jnp.float32)),
        in_specs=[hbm] * 5,
        out_specs=(vmem, vmem),
        scratch_shapes=[
            pltpu.VMEM((points, lat), jnp.bfloat16),
            pltpu.VMEM((nvar, lat), jnp.bfloat16),
            pltpu.VMEM((padded, lat), jnp.bfloat16),
            pltpu.VMEM((CHUNKS, nvar, width), jnp.float32),
            pltpu.VMEM((points // LANES, LANES), jnp.float32),
            pltpu.VMEM((1, nvar), jnp.float32),
            pltpu.VMEM((LANES, LANES), jnp.float32),
            pltpu.VMEM((CHUNKS, count, packed, LANES), jnp.bfloat16),
            pltpu.VMEM((CHUNKS, count, packed, LANES), jnp.bfloat16),
            pltpu.VMEM((CHUNKS, count, packed, LANES), jnp.bfloat16),
            pltpu.VMEM((CHUNKS, count, packed, LANES), jnp.bfloat16),
            pltpu.VMEM((CHUNKS, padded, points // CHUNKS), jnp.bfloat16),
            pltpu.VMEM((LANES, lat), jnp.float32),
            pltpu.VMEM((2, shards // 2, share, LANES), jnp.float32),
            pltpu.VMEM((shards // 2, share, LANES), jnp.float32),
            pltpu.VMEM((shards // 2, share, LANES), jnp.float32),
            pltpu.VMEM((shards, share // 2, LANES), jnp.float32),
            pltpu.VMEM((count, share // 2, LANES), jnp.float32),
            dma((CHUNKS,)),
            dma((count,)),
            dma((CHUNKS,)),
            dma((3,)),
            dma((CHUNKS,)),
            dma((CHUNKS,)),
            dma((CHUNKS,)),
            dma((CHUNKS, 2)),
            dma,
            dma,
            dma,
            dma,
            dma,
            dma,
        ],
        compiler_params=pltpu.CompilerParams(
            collective_id=0, has_side_effects=True, vmem_limit_bytes=36 * 2**20
        ),
        name="crps_step",
    )(
        *(
            pltpu.with_memory_space_constraint(x, pltpu.HBM)
            for x in (
                latent,
                proj_weight.T,
                truth,
                area_weight.reshape(points // LANES, LANES),
                var_weight.reshape(1, nvar),
            )
        )
    )
    latent_grad, weight_grad, loss = pl.pallas_call(
        functools.partial(copy_out, sizes),
        out_shape=out_shape,
        in_specs=[vmem, vmem],
        out_specs=(hbm, hbm, hbm),
        scratch_shapes=[
            pltpu.VMEM((share, nvar), jnp.float32),
            pltpu.VMEM((1, 1), jnp.float32),
            dma((3,)),
        ],
        compiler_params=pltpu.CompilerParams(vmem_limit_bytes=2**20),
        name="copy_out",
    )(*(pltpu.with_memory_space_constraint(x, pltpu.VMEM) for x in (latent_grad, summed)))
    return (loss[0, 0], latent_grad, weight_grad)


def solution(mesh):
    placed = (P("ens", "grid", None), P(), P(None, "grid"), P("grid"), P())
    return jax.shard_map(
        per_device,
        mesh=mesh,
        in_specs=placed,
        out_specs=(P(), P("ens", "grid", None), P("grid", None)),
        check_vma=False,
    )
```
